32 devices in a mesh: comp: 2 (over y), gy: 4 (over z), gx: 4 (over x, core).
Axes of the slice: x: 2, y: 2, z: 4, core: 2. Of those that a mesh axis runs over, the one named last changes fastest.
Arguments:
- spectra: float32 [32, 36, 16, 512], P('comp', None, 'gy', 'gx'), may hold values from 0.05 to 2
- wind_field: float32 [2, 16, 512], P(None, 'gy', 'gx'), may hold values from -5 to 5
- sea_mask: int32 [16, 512], P('gy', 'gx'), may hold values 0 or 1
- first_layer: bfloat16 [1152, 1024], replicated, may hold values from -0.1875 to 0.1875
- second_layer: bfloat16 [1024, 1152], replicated, may hold values from -0.1875 to 0.1875
- ocean_state: float32 [4, 16, 16, 512], P(None, None, 'gy', 'gx'), may hold values from -4 to 4
- current_blocks: float32 [16, 2, 512, 128], P('gy', None, 'gx'), may hold values from 0 to 1
- current_rows: int32 [16, 2, 4], P('gy', None, 'gx'), may hold values from 0 to 15, as said below
- stress_blocks: float32 [16, 2, 512, 128], P('gy', None, 'gx'), may hold values from 0 to 1
- stress_rows: int32 [16, 2, 4], P('gy', None, 'gx'), may hold values from 0 to 15, as said below
Outputs:
- spectra_next: float32 [32, 36, 16, 512], P('comp', None, 'gy', 'gx')
- ocean_next: float32 [4, 16, 16, 512], P(None, None, 'gy', 'gx')
The draws below stay inside these ranges and needn't reach their ends.
Inputs may be any that keep to these rules, and one draw needn't show every extreme that they name: `current_rows`: entry [r, b, t] is the source row read by block b of destination row r in column tile t; it lies within one row of r, and both r - 1 and r + 1 occur. `stress_rows`: entry [r, b, t] is the source row read by block b of destination row r in column tile t; it lies within one row of r, and both r - 1 and r + 1 occur.
All inputs are finite; a program needn't handle non-finite values. No bound on the sum of `sea_mask` on one device may be relied on, other than what follows from the above.
Results may differ from the reference program's by a relative error of at most 0.0023.
Values may be sent and summed in bfloat16 or wider, within the bound.
A program may use at most 64 MiB of HBM per device.

```python
import math
import jax
import jax.numpy as jnp
from jax import lax

FREQS = 32
DIRS = 36
HID = 1024
LEV = 16
STEPS = 2
NB = 2
COLS_DEV = 128
NLAT = 16
NLON = 512
TILES_X = 4
K = 1152


def block_weights(key, salt_value):
    folded = jax.random.fold_in(key, salt_value)
    spread_key = jax.random.fold_in(folded, 1)
    diag_key = jax.random.fold_in(folded, 2)
    spread_part = jax.random.uniform(spread_key, (NLAT, NB, NLON, COLS_DEV), jnp.float32, 0.0, 3.0 / COLS_DEV)
    diag_scale = jax.random.uniform(diag_key, (NLAT, NB, NLON, COLS_DEV), jnp.float32, 0.1, 0.6)
    column_pos = jnp.arange(NLON) % COLS_DEV
    diagonal = (column_pos[:, None] == jnp.arange(COLS_DEV)[None, :]).astype(jnp.float32)
    return diagonal[None, None, :, :] * diag_scale + spread_part


def source_table(key, salt_value):
    folded = jax.random.fold_in(key, salt_value)
    offsets = jax.random.randint(folded, (NLAT, NB, TILES_X), -1, 2)
    row_pos = jnp.arange(NLAT)[:, None, None]
    block_pos = jnp.arange(NB)[None, :, None]
    row_table = jnp.clip(row_pos + offsets, 0, NLAT - 1)
    row_table = jnp.where((row_pos == 0) & (block_pos == 0), 0, row_table)
    row_table = jnp.where((row_pos == NLAT - 1) & (block_pos == 0), NLAT - 1, row_table)
    row_table = jnp.where((row_pos == 1) & (block_pos == 0), 0, row_table)
    row_table = jnp.where((row_pos == NLAT - 2) & (block_pos == 0), NLAT - 1, row_table)
    return row_table.astype(jnp.int32)


def draw_current_blocks(key, part):
    return block_weights(key, 11)


def draw_stress_blocks(key, part):
    return block_weights(key, 23)


def draw_current_rows(key, part):
    return source_table(key, 37)


def draw_stress_rows(key, part):
    return source_table(key, 41)


def place_ends(values, rng, smallest, largest):
    longest = values.shape.index(max(values.shape))
    spots = []
    for shift in (0, 1):
        where = [jax.random.randint(jax.random.fold_in(rng, axis), (), 0, length) for axis, length in enumerate(values.shape)]
        where[longest] = (where[longest] + shift) % values.shape[longest]
        spots.append(tuple(where))
    return values.at[spots[0]].set(smallest).at[spots[1]].set(largest)


def block_scale(rng, dims, cuts, smallest, top_value):
    loudness, own = 1.0, jax.random.fold_in(rng, 6)
    for axis_at, shards_of in cuts:
        steps = jnp.exp(jax.random.uniform(jax.random.fold_in(own, axis_at), (shards_of,), jnp.float32, smallest / len(cuts), top_value / len(cuts)))
        loudness = loudness * jnp.repeat(steps, dims[axis_at] // shards_of).reshape([-1 if axis == axis_at else 1 for axis in range(len(dims))])
    return loudness


def noise(own_key, extent, scale, bound, shards=(), kind=jnp.bfloat16):
    factor_of = block_scale(own_key, extent, shards, -0.22, 0.18) if shards else 1.0
    entries = jax.random.normal(own_key, extent, jnp.float32) * scale * factor_of
    return jnp.minimum(jnp.maximum(entries, -bound), bound).astype(kind)


def setup_inputs(seed: int = 0) -> dict:
    keys = jax.random.split(jax.random.key(seed), 11)
    spectra = jnp.clip(jnp.exp(math.log(2.0) - 3.6888794 * jax.random.uniform(keys[0], (FREQS, DIRS, NLAT, NLON), jnp.float32) ** block_scale(keys[0], (FREQS, DIRS, NLAT, NLON), ((0, 2), (2, 4), (3, 4)), -0.2, 0.2)), 0.05, 2.0)
    wind_field = noise(keys[1], (2, NLAT, NLON), 2.0, 5.0, ((1, 4), (2, 4)), jnp.float32)
    sea_mask = place_ends((jax.random.randint(keys[2], (NLAT, NLON), 0, 10) < 9).astype(jnp.int32), jax.random.fold_in(keys[2], 1), 0, 1)
    first_layer = noise(keys[3], (K, HID), K ** -0.5, 0.1875)
    second_layer = noise(keys[4], (HID, K), HID ** -0.5, 0.1875)
    ocean_state = noise(keys[5], (4, LEV, NLAT, NLON), 1.0, 4.0, ((2, 4), (3, 4)), jnp.float32)
    current_blocks = draw_current_blocks(jax.random.fold_in(keys[10], 71), 0)
    current_rows = draw_current_rows(jax.random.fold_in(keys[10], 71), 0)
    stress_blocks = draw_stress_blocks(jax.random.fold_in(keys[10], 71), 0)
    stress_rows = draw_stress_rows(jax.random.fold_in(keys[10], 71), 0)
    return {"spectra": spectra, "wind_field": wind_field, "sea_mask": sea_mask, "first_layer": first_layer, "second_layer": second_layer, "ocean_state": ocean_state, "current_blocks": current_blocks, "current_rows": current_rows, "stress_blocks": stress_blocks, "stress_rows": stress_rows}


CURRENT_GAIN = 0.08
WIND_GAIN = 0.06
DECAY_GAIN = 0.03
NONLINEAR_GAIN = 0.3
THERMAL = 0.2
HALINE = 0.8
CORIOLIS = 0.1
PRESSURE_GAIN = 0.2
LATERAL_MIX = 0.1
VERTICAL_MIX = 0.2
ADVECTION = 0.3
STRESS_GAIN = 150.0


def spectral_tables(first, count, total, directions):
    freq_index = (jnp.arange(count) + first).astype(jnp.float32)
    group_speed = 0.4 * jnp.exp(-3.0 * freq_index / (total - 1))
    phase_speed = 4.0 * group_speed
    freq_ratio = jnp.exp(2.0 * freq_index / (total - 1) - 1.0)
    angles = 2.0 * jnp.pi * jnp.arange(directions).astype(jnp.float32) / directions
    return group_speed, phase_speed, freq_ratio, jnp.cos(angles), jnp.sin(angles)


def advect(spectrum, padded, group_speed, cosines, sines, currents, mask_f):
    western = padded[:, :, 1:-1, :-2]
    eastern = padded[:, :, 1:-1, 2:]
    southern = padded[:, :, :-2, 1:-1]
    northern = padded[:, :, 2:, 1:-1]
    speed_x = group_speed[:, None, None, None] * cosines[None, :, None, None] + CURRENT_GAIN * currents[0]
    speed_y = group_speed[:, None, None, None] * sines[None, :, None, None] + CURRENT_GAIN * currents[1]
    flux_sum = jnp.maximum(speed_x, 0.0) * (spectrum - western) + jnp.minimum(speed_x, 0.0) * (eastern - spectrum)
    flux_sum = flux_sum + jnp.maximum(speed_y, 0.0) * (spectrum - southern) + jnp.minimum(speed_y, 0.0) * (northern - spectrum)
    return mask_f * (spectrum - flux_sum)


def source_rates(propagated, wind_field, phase_speed, freq_ratio, cosines, sines):
    growth = WIND_GAIN * jnp.maximum(wind_field[0] * cosines[None, :, None, None] + wind_field[1] * sines[None, :, None, None] - phase_speed[:, None, None, None], 0.0)
    energy = jnp.sum(propagated, axis=(0, 1))
    moment = jnp.sum(freq_ratio[:, None, None, None] * propagated, axis=(0, 1))
    push_x = jnp.sum(growth * propagated * cosines[None, :, None, None], axis=(0, 1))
    push_y = jnp.sum(growth * propagated * sines[None, :, None, None], axis=(0, 1))
    return growth, (energy, moment, push_x, push_y)


def contract(left, right):
    return lax.dot_general(left, right, (((0,), (0,)), ((), ())), preferred_element_type=jnp.float32)


def ocean_update(padded, stress, mask_f):
    def middle(field):
        return field[..., 1:-1, 1:-1]

    def eastern(field):
        return field[..., 1:-1, 2:]

    def western(field):
        return field[..., 1:-1, :-2]

    def northern(field):
        return field[..., 2:, 1:-1]

    def southern(field):
        return field[..., :-2, 1:-1]

    def spread(field):
        return eastern(field) + western(field) + northern(field) + southern(field) - 4.0 * middle(field)

    def column(field):
        upper_level = jnp.concatenate([field[:1], field[:-1]], axis=0)
        lower_level = jnp.concatenate([field[1:], field[-1:]], axis=0)
        return upper_level + lower_level - 2.0 * field

    density = -THERMAL * padded[2] + HALINE * padded[3]
    pressure = jnp.cumsum(density, axis=0) - 0.5 * density
    speed_u = middle(padded[0])
    speed_v = middle(padded[1])

    def carry_term(field):
        return speed_u * 0.5 * (eastern(field) - western(field)) + speed_v * 0.5 * (northern(field) - southern(field))

    surface = (jnp.arange(padded.shape[1]) == 0).astype(jnp.float32)[:, None, None]
    tend_u = CORIOLIS * speed_v - PRESSURE_GAIN * 0.5 * (eastern(pressure) - western(pressure)) + LATERAL_MIX * spread(padded[0]) + VERTICAL_MIX * column(speed_u) + STRESS_GAIN * surface * stress[0]
    tend_v = -CORIOLIS * speed_u - PRESSURE_GAIN * 0.5 * (northern(pressure) - southern(pressure)) + LATERAL_MIX * spread(padded[1]) + VERTICAL_MIX * column(speed_v) + STRESS_GAIN * surface * stress[1]
    tend_t = -ADVECTION * carry_term(padded[2]) + LATERAL_MIX * spread(padded[2]) + VERTICAL_MIX * column(middle(padded[2]))
    tend_s = -ADVECTION * carry_term(padded[3]) + LATERAL_MIX * spread(padded[3]) + VERTICAL_MIX * column(middle(padded[3]))
    return middle(padded) + mask_f * jnp.stack([tend_u, tend_v, tend_t, tend_s])


def regrid(field, blocks, row_table):
    tiled = field.reshape(2, NLAT, TILES_X, COLS_DEV).transpose(0, 2, 1, 3)
    tile_index = jnp.arange(TILES_X)[None, None, :]
    selected = tiled[:, tile_index, row_table, :]
    weights = blocks.reshape(NLAT, NB, TILES_X, COLS_DEV, COLS_DEV)
    result = jnp.einsum("rbtds,krbts->krtd", weights, selected, precision=lax.Precision.HIGHEST)
    return result.reshape(2, NLAT, NLON)


def reference(spectra, wind_field, sea_mask, first_layer, second_layer, ocean_state, current_blocks, current_rows, stress_blocks, stress_rows):
    mask_f = sea_mask.astype(jnp.float32)
    currents = regrid(jnp.stack([ocean_state[0, 0], ocean_state[1, 0]]), current_blocks, current_rows)
    group_speed, phase_speed, freq_ratio, cosines, sines = spectral_tables(0, FREQS, FREQS, DIRS)
    spectrum = spectra
    stress_sum = jnp.zeros((2, NLAT, NLON), jnp.float32)

    def network(row_block):
        hidden = jax.nn.silu(contract(first_layer, row_block)).astype(jnp.bfloat16)
        return contract(second_layer, hidden).astype(jnp.bfloat16)

    for step_index in range(STEPS):
        padded = jnp.pad(spectrum, ((0, 0), (0, 0), (1, 1), (1, 1)))
        propagated = advect(spectrum, padded, group_speed, cosines, sines, currents, mask_f)
        growth, partials = source_rates(propagated, wind_field, phase_speed, freq_ratio, cosines, sines)
        energy, moment, push_x, push_y = partials
        energy_floor = jnp.maximum(energy, 1.0)
        scaled = (propagated * (K / energy_floor)).astype(jnp.bfloat16)
        by_rows = jnp.transpose(scaled, (2, 0, 1, 3)).reshape(NLAT, K, NLON)
        transfer = lax.map(network, by_rows).reshape(NLAT, FREQS, DIRS, NLON).transpose(1, 2, 0, 3)
        damping = DECAY_GAIN * freq_ratio[:, None, None, None] * (moment / energy_floor) ** 2
        spectrum = propagated * jnp.exp(growth - damping) + NONLINEAR_GAIN * (energy_floor / K) * transfer.astype(jnp.float32)
        stress_sum = stress_sum + jnp.stack([push_x, push_y]) / K
    stress_ocean = regrid(stress_sum / STEPS, stress_blocks, stress_rows)
    padded_ocean = jnp.pad(ocean_state, ((0, 0), (0, 0), (1, 1), (1, 1)))
    return spectrum, ocean_update(padded_ocean, stress_ocean, mask_f)
```

```python
import numpy as np

import jax
import jax.numpy as jnp
from jax import lax
from jax.experimental import pallas as pl
from jax.experimental.pallas import tpu as pltpu
from jax.sharding import PartitionSpec as P

CURRENT_GAIN = 0.08
WIND_GAIN = 0.06
DECAY_GAIN = 0.03
NONLINEAR_GAIN = 0.3
THERMAL = 0.2
HALINE = 0.8
CORIOLIS = 0.1
PRESSURE_GAIN = 0.2
LATERAL_MIX = 0.1
VERTICAL_MIX = 0.2
ADVECTION = 0.3
STRESS_GAIN = 150.0

STEPS = 2
ROWS = 4
COLS = 128
HALF = 64
CELLS = ROWS * HALF
TILE = 128
TILES = 9
OWN = 4
PAD = 8
GROUPS = ((0, 1), (5, 6), (4,), (2, 3), (7, 8))
SENDERS = (1, 0, 2, 4, 3)
LAST_GROUPS = ((5, 6), (7, 8), (4,), (0, 1), (2, 3))
VMEM_LIMIT = 56 * 1024 * 1024


def tables(total, directions):
    index = np.arange(total, dtype=np.float64)
    group = 0.4 * np.exp(-3.0 * index / (total - 1))
    ratio = np.exp(2.0 * index / (total - 1) - 1.0)
    angles = 2.0 * np.pi * np.arange(directions) / directions
    cosines, sines = np.cos(angles), np.sin(angles)
    full = np.zeros((8, total, directions))
    full[0] = group[:, None] * cosines
    full[1] = group[:, None] * sines
    full[2] = cosines
    full[3] = sines
    full[4] = WIND_GAIN * 4.0 * group[:, None]
    full[5] = ratio[:, None]
    tiled = full.reshape(8, TILES, TILE).transpose(1, 0, 2)
    swapped = np.concatenate([tiled[5:], tiled[4:5], tiled[:4]])
    return np.stack([tiled, swapped]).astype(np.float32)


def mirror(t):
    return 4 if t == 4 else (t + 5) % 10


def kernel(
    spectra, first, second, table, ocean, wind, mask, cblocks, sblocks, crows, srows,
    out, o_out,
    spec, w1, w2, tab, oc, wnd, msk, cb, sb,
    state, prop, rate, p16, part, hidden, sums, cells, gain, back, squared, small, small_t,
    y_out, y_in, z1_out, z1_in, zf_in, es_out, es_in, ed_out, ed_in, ep_out, ep_in, el,
    z2_out, z2_in, e2d_out, e2d_in, e2p_out, e2p_in,
    oz_out, oz_in, ocat, ox_out, ox_in, st_out, st_in, st_full, sz_in, f_out, f_in,
    load, oz_send, oz_recv, ox_send, ox_recv, y_send, y_recv, z1_send, z1_recv,
    zf_send, zf_recv, e1_send, e1_recv, z2_send, z2_recv, e2_send, e2_recv,
    s_send, s_recv, f_send, f_recv,
):
    f32, b16 = jnp.float32, jnp.bfloat16
    me = lax.axis_index("comp")
    other = 1 - me
    gy, ny = lax.axis_index("gy"), lax.axis_size("gy")
    gx, nx = lax.axis_index("gx"), lax.axis_size("gx")
    comps = spectra.shape[0]
    mesh_ids = pl.DeviceIdType.MESH

    def local(source, target, n):
        return pltpu.make_async_copy(source, target, load.at[n])

    own_at = pl.multiple_of(me * 5 * TILE, TILE)
    far_at = pl.multiple_of(other * 5 * TILE, TILE)
    half_at = pl.multiple_of(me * HALF, HALF)
    spec_load = local(spectra, spec.at[pl.ds(HALF, comps)], 0)
    ocean_load = local(ocean, oc, 1)
    wind_load = local(wind, wnd, 2)
    mask_load = local(mask, msk, 3)
    table_load = local(table.at[me], tab, 4)
    cb_load = local(cblocks.at[:, :, pl.ds(half_at, HALF), :], cb, 5)
    sb_load = local(sblocks, sb, 6)
    w1_loads = [
        local(first.at[pl.ds(own_at, 512)], w1.at[pl.ds(0, 512)], 7),
        local(first.at[pl.ds(512, 128)], w1.at[pl.ds(512, 128)], 8),
        local(first.at[pl.ds(far_at, 512)], w1.at[pl.ds(640, 512)], 9),
    ]
    w2_loads = [
        local(second.at[:, pl.ds(own_at, 512)], w2.at[:, pl.ds(0, 512)], 10),
        local(second.at[:, pl.ds(512, 128)], w2.at[:, pl.ds(512, 128)], 11),
        local(second.at[:, pl.ds(far_at, 512)], w2.at[:, pl.ds(640, 512)], 12),
    ]
    all_loads = [ocean_load, spec_load, wind_load, mask_load, table_load, cb_load]
    all_loads += w1_loads + w2_loads + [sb_load]
    for copy in all_loads:
        copy.start()

    for ref in (es_in, ed_in, e2d_in, sz_in, ox_in, oz_in):
        ref[...] = jnp.zeros_like(ref)

    has_s, has_n = gy > 0, gy < ny - 1
    has_w, has_e = gx > 0, gx < nx - 1
    south = {"gy": lax.rem(gy + ny - 1, ny)}
    north = {"gy": lax.rem(gy + 1, ny)}
    west = {"gx": lax.rem(gx + nx - 1, nx)}
    east = {"gx": lax.rem(gx + 1, nx)}
    pair = {"comp": other}
    far_gx = gx + 2 * me - 1
    has_far = jnp.logical_and(far_gx >= 0, far_gx < nx)
    diag = {"comp": other, "gx": lax.rem(far_gx + nx, nx)}
    same_gx = gx + 1 - 2 * me
    has_same = jnp.logical_and(same_gx >= 0, same_gx < nx)
    same = {"gx": lax.rem(same_gx + nx, nx)}

    barrier = pltpu.get_barrier_semaphore()
    greet = ((has_s, south), (has_n, north), (has_w, west), (has_e, east), (has_far, diag))
    for there, place in greet:
        @pl.when(there)
        def _(place=place):
            pl.semaphore_signal(barrier, inc=1, device_id=place, device_id_type=mesh_ids)
    pl.semaphore_signal(barrier, inc=1, device_id=pair, device_id_type=mesh_ids)

    def remote(source, target, send, recv, where):
        return pltpu.make_async_remote_copy(
            src_ref=source, dst_ref=target, send_sem=send, recv_sem=recv,
            device_id=where, device_id_type=mesh_ids,
        )

    ocean_n = remote(oz_out.at[0], oz_in.at[0], oz_send.at[0], oz_recv.at[0], north)
    ocean_s = remote(oz_out.at[1], oz_in.at[1], oz_send.at[1], oz_recv.at[1], south)
    ocean_e = remote(
        ox_out.at[pl.ds(120, 8)], ox_in.at[0, pl.ds(120, 8)], ox_send.at[0], ox_recv.at[0], east
    )
    ocean_w = remote(
        ox_out.at[pl.ds(0, 8)], ox_in.at[1, pl.ds(0, 8)], ox_send.at[1], ox_recv.at[1], west
    )
    swap = [
        remote(y_out.at[r], y_in.at[r], y_send.at[r], y_recv.at[r], pair) for r in range(ROWS)
    ]
    z1_n = remote(z1_out.at[0], z1_in.at[0], z1_send.at[0], z1_recv.at[0], north)
    z1_s = remote(z1_out.at[1], z1_in.at[1], z1_send.at[1], z1_recv.at[1], south)
    zf_n = remote(y_in.at[ROWS - 1], zf_in.at[0], zf_send.at[0], zf_recv.at[0], north)
    zf_s = remote(y_in.at[0], zf_in.at[1], zf_send.at[1], zf_recv.at[1], south)
    e_same = remote(es_out, es_in, e1_send.at[0], e1_recv.at[0], same)
    e_diag = remote(ed_out, ed_in, e1_send.at[1], e1_recv.at[1], diag)
    e_pair = remote(ep_out, ep_in, e1_send.at[2], e1_recv.at[2], pair)

    def span(tiles):
        return pl.ds(tiles[0], len(tiles))

    z2 = []
    e2 = []
    for g, tiles in enumerate(GROUPS):
        part_of = span(tiles)
        z2.append([
            remote(
                z2_out.at[d, part_of], z2_in.at[d, part_of],
                z2_send.at[d, g], z2_recv.at[d, g], (north, south)[d],
            )
            for d in range(2)
        ])
        there = span(tuple(sorted(mirror(t) for t in tiles)))
        e2.append([
            remote(
                e2d_out.at[part_of], e2d_in.at[there], e2_send.at[0, g], e2_recv.at[0, g], diag
            ),
            remote(
                e2p_out.at[part_of], e2p_in.at[there], e2_send.at[1, g], e2_recv.at[1, g], pair
            ),
        ])
    stress_pair = remote(st_out, st_in, s_send.at[0], s_recv.at[0], pair)
    stress_n = remote(st_full, sz_in.at[0], s_send.at[1], s_recv.at[1], north)
    stress_s = remote(st_full, sz_in.at[1], s_send.at[2], s_recv.at[2], south)
    final_parts = (pl.ds(0, 2), pl.ds(2, 2), pl.ds(4, 1))
    final = [
        remote(f_out.at[p], f_in.at[p], f_send.at[n], f_recv.at[n], pair)
        for n, p in enumerate(final_parts)
    ]

    def when(condition, *actions):
        @pl.when(condition)
        def _():
            for action in actions:
                action()

    state[...] = jnp.zeros_like(state)
    spec[:HALF] = jnp.zeros((HALF, ROWS, COLS), f32)
    spec[HALF + comps :] = jnp.zeros((HALF, ROWS, COLS), f32)

    ocean_load.wait()
    oz_out[0] = oc[:, ROWS - 1, :]
    oz_out[1] = oc[:, 0, :]
    for r in range(ROWS):
        ocat[64 * r : 64 * (r + 1), :] = oc[:, r, :]
    ox_out[...] = ocat[...].T
    counted = [jnp.where(there, 1, 0) for there, _ in greet]
    pl.semaphore_wait(barrier, 1 + sum(counted))
    when(has_n, ocean_n.start)
    when(has_s, ocean_s.start)

    half_is0 = jnp.broadcast_to(me, (HALF, TILE)) == 0
    row_is0 = jnp.broadcast_to(me, (1, TILE)) == 0
    lane = lax.broadcasted_iota(jnp.int32, (HALF, TILE), 1)
    mine = jnp.where(lane < 64, 0, 1) == me
    mine_row = mine[:1]
    starts = [HALF + me * HALF + TILE * t for t in range(OWN)] + [other * (comps + HALF - 64)]
    spec_load.wait()
    for r in (3, 0, 1, 2):
        for t in range(OWN + 1):
            turned = spec[pl.ds(starts[t], TILE), r, :].T
            low, high = turned[:HALF], turned[HALF:]
            own = jnp.where(half_is0, low, high)
            state[t, r + 1, PAD : PAD + HALF] = own
            y_out[r, t] = jnp.where(half_is0, high, low).astype(b16)
            if r == 3:
                z1_out[0, t] = own.astype(b16)
            if r == 0:
                z1_out[1, t] = own.astype(b16)
            es_out[t, r : r + 1] = jnp.where(row_is0, turned[127:128], turned[0:1])
            ed_out[t, r : r + 1] = jnp.where(row_is0, turned[0:1], turned[127:128])
            ep_out[t, r : r + 1] = jnp.where(row_is0, turned[63:64], turned[64:65])
            el[t, r : r + 1] = jnp.where(row_is0, turned[64:65], turned[63:64])
        swap[r].start()
        if r == 3:
            when(has_n, z1_n.start)
        if r == 0:
            when(has_s, z1_s.start)
    when(has_same, e_same.start)
    when(has_far, e_diag.start)
    e_pair.start()
    when(has_e, ocean_e.start)
    when(has_w, ocean_w.start)

    wind_load.wait()
    mask_load.wait()
    table_load.wait()
    small[...] = jnp.zeros_like(small)
    small[0:4] = msk[...].astype(f32)
    small[4:8] = WIND_GAIN * wnd[0]
    small[8:12] = WIND_GAIN * wnd[1]
    small_t[...] = small[...].T
    columns = small_t[pl.ds(half_at, HALF), :]
    for q in range(3):
        for r in range(ROWS):
            n = 4 * q + r
            cells[2 + q, HALF * r : HALF * (r + 1), :] = jnp.broadcast_to(
                columns[:, n : n + 1], (HALF, TILE)
            )
    cb_load.wait()
    when(has_s, ocean_n.wait_recv)
    when(has_n, ocean_s.wait_recv)

    def choose(rows_ref, r, b, below, here, above):
        offset = jnp.broadcast_to(rows_ref[r, b, 0] - gy * ROWS - r, (1, COLS))
        return jnp.where(offset < 0, below, jnp.where(offset == 0, here, above))

    for k in range(2):
        at = 16 * k
        lines = [oz_in[0, at : at + 1]]
        lines += [oc[at : at + 1, r, :] for r in range(ROWS)]
        lines += [oz_in[1, at : at + 1]]
        for r in range(ROWS):
            total = cb[r, 0] * choose(crows, r, 0, *lines[r : r + 3])
            total = total + cb[r, 1] * choose(crows, r, 1, *lines[r : r + 3])
            cells[k, HALF * r : HALF * (r + 1), :] = jnp.broadcast_to(
                CURRENT_GAIN * total.sum(axis=1, keepdims=True), (HALF, TILE)
            )

    def edges(t, pair_side, far_side):
        for r in range(ROWS):
            near, far = pair_side[r : r + 1], far_side[r : r + 1]
            state[t, r + 1, PAD - 1 : PAD] = jnp.where(row_is0, far, near)
            state[t, r + 1, PAD + HALF : PAD + HALF + 1] = jnp.where(row_is0, near, far)

    def propagate(tiles, fresh, fresh_push):
        def body(r, carry):
            at = pl.multiple_of(r * HALF, HALF)
            for lo in (0, 32):
                cell = pl.ds(at + lo, 32)
                cur_x, cur_y, wet, wind_x, wind_y = (cells[q, cell, :] for q in range(5))
                zero = jnp.zeros((32, TILE), f32)
                totals = [
                    zero if (fresh if q < 2 else fresh_push) else sums[q, cell, :]
                    for q in range(4)
                ]
                for t in tiles:
                    speed_x, speed_y, cos, sin, phase, ratio = (
                        tab[t, q : q + 1, :] for q in range(6)
                    )
                    top = PAD + lo
                    here = state[t, r + 1, top : top + 32]
                    before = state[t, r + 1, top - 1 : top + 31]
                    after = state[t, r + 1, top + 1 : top + 33]
                    below = state[t, r, top : top + 32]
                    above = state[t, r + 2, top : top + 32]
                    cx = speed_x + cur_x
                    cy = speed_y + cur_y
                    flux = jnp.abs(cx) * (here - jnp.where(cx > 0.0, before, after))
                    flux = flux + jnp.abs(cy) * (here - jnp.where(cy > 0.0, below, above))
                    moved = wet * (here - flux)
                    growth = jnp.maximum(wind_x * cos + wind_y * sin - phase, 0.0)
                    pushed = growth * moved
                    prop[t, cell, :] = moved
                    rate[t, cell, :] = growth
                    p16[cell, TILE * t : TILE * (t + 1)] = moved.astype(b16)
                    parts = (moved, ratio * moved, pushed * cos, pushed * sin)
                    totals = [a + b for a, b in zip(totals, parts)]
                for q in range(4):
                    sums[q, cell, :] = totals[q]
            return carry

        lax.fori_loop(0, ROWS, body, 0)

    def finish_sums():
        total = STEPS * comps

        def spread(ref):
            return jnp.broadcast_to(ref.sum(axis=1, keepdims=True), (CELLS, TILE))

        floor = jnp.maximum(spread(sums[0]), 1.0)
        share = spread(sums[1]) / floor
        squared[...] = DECAY_GAIN * share * share
        gain[...] = (0.5 * total) / floor
        back[...] = (NONLINEAR_GAIN / total) * floor

    def dot(left, right):
        return lax.dot_general(
            left, right, (((1,), (0,)), ((), ())), preferred_element_type=f32
        )

    def activate(n, pre):
        for j in range(2):
            half = pre[:, TILE * j : TILE * (j + 1)] * gain[...]
            at = 256 * n + TILE * j
            hidden[:, at : at + TILE] = (half + half * jnp.tanh(half)).astype(b16)

    def update(tiles):
        at = TILE * tiles[0]
        moved = dot(hidden[...], w2[:, at : at + TILE * len(tiles)])
        for j, t in enumerate(tiles):
            transfer = moved[:, TILE * j : TILE * (j + 1)].astype(b16).astype(f32)
            fresh = prop[t] * jnp.exp(rate[t] - tab[t, 5:6, :] * squared[...])
            fresh = fresh + back[...] * transfer
            yield t, fresh

    when(has_s, z1_n.wait_recv)
    when(has_n, z1_s.wait_recv)
    when(has_far, e_same.wait_recv)
    for t in range(OWN):
        edges(t, el[t], es_in[t])
    for d, there in ((0, has_s), (1, has_n)):
        @pl.when(there)
        def _(d=d):
            for t in range(OWN):
                state[t, 5 * d, PAD : PAD + HALF] = z1_in[d, t].astype(f32)
    propagate(range(OWN), True, True)
    swap[3].wait_recv()
    when(has_n, zf_n.start)
    swap[0].wait_recv()
    when(has_s, zf_s.start)
    for copy in w1_loads:
        copy.wait()
    for n in range(4):
        lanes = slice(256 * n, 256 * (n + 1))
        part[:, lanes] = dot(p16[:, : TILE * OWN], w1[: TILE * OWN, lanes])

    when(has_w, ocean_e.wait_recv)
    when(has_e, ocean_w.wait_recv)
    from_w, from_e = ox_in[0].T, ox_in[1].T
    lane64 = lax.broadcasted_iota(jnp.int32, (64, COLS), 1)
    level64 = lax.rem(lax.broadcasted_iota(jnp.int32, (64, COLS), 0), 16)
    level = lax.broadcasted_iota(jnp.int32, (16, COLS), 0)

    def density(field):
        return HALINE * field[48:64] - THERMAL * field[32:48]

    def pressure(dense):
        running = dense
        for shift in (1, 2, 4, 8):
            running = running + jnp.where(level >= shift, pltpu.roll(running, shift, 0), 0.0)
        return running - 0.5 * dense

    for r in range(ROWS):
        here = oc[:, r, :]
        low = oz_in[0] if r == 0 else oc[:, r - 1, :]
        high = oz_in[1] if r == ROWS - 1 else oc[:, r + 1, :]
        lines = slice(64 * r, 64 * (r + 1))
        left = pltpu.roll(jnp.where(lane64 == COLS - 1, from_w[lines], here), 1, 1)
        right = pltpu.roll(jnp.where(lane64 == 0, from_e[lines], here), COLS - 1, 1)
        upper = jnp.where(level64 == 0, here, pltpu.roll(here, 1, 0))
        lower = jnp.where(level64 == 15, here, pltpu.roll(here, 63, 0))
        mixed = LATERAL_MIX * (left + right + low + high - 4.0 * here)
        mixed = mixed + VERTICAL_MIX * (upper + lower - 2.0 * here)
        across, along = right - left, high - low
        speed_u, speed_v = here[0:16], here[16:32]
        half_gain = 0.5 * PRESSURE_GAIN
        du = CORIOLIS * speed_v - half_gain * pressure(density(across))
        dv = -CORIOLIS * speed_u - half_gain * pressure(density(along))
        pull = -0.5 * ADVECTION
        dtemp = pull * (speed_u * across[32:48] + speed_v * along[32:48])
        dsalt = pull * (speed_u * across[48:64] + speed_v * along[48:64])
        tendency = mixed + jnp.concatenate([du, dv, dtemp, dsalt], axis=0)
        o_out[:, r, :] = here + msk[r : r + 1, :].astype(f32) * tendency

    swap[1].wait_recv()
    swap[2].wait_recv()
    for r in range(ROWS):
        for t in range(OWN):
            state[5 + t, r + 1, PAD : PAD + HALF] = y_in[r, t].astype(f32)
        state[4, r + 1, PAD : PAD + HALF] = jnp.where(
            mine, state[4, r + 1, PAD : PAD + HALF], y_in[r, 4].astype(f32)
        )
    when(has_far, e_diag.wait_recv)
    e_pair.wait_recv()
    for t in range(OWN):
        edges(5 + t, ep_in[t], ed_in[t])
    edges(4, jnp.where(mine[:8], el[4], ep_in[4]), jnp.where(mine[:8], es_in[4], ed_in[4]))
    for d, there, copy in ((0, has_s, zf_n), (1, has_n, zf_s)):
        @pl.when(there)
        def _(d=d, copy=copy):
            copy.wait_recv()
            for t in range(OWN):
                state[5 + t, 5 * d, PAD : PAD + HALF] = zf_in[d, t].astype(f32)
            state[4, 5 * d, PAD : PAD + HALF] = jnp.where(
                mine, z1_in[d, 4].astype(f32), zf_in[d, 4].astype(f32)
            )
    propagate(range(OWN, TILES), False, False)
    finish_sums()
    for n in range(4):
        lanes = slice(256 * n, 256 * (n + 1))
        activate(n, part[:, lanes] + dot(p16[:, TILE * OWN :], w1[TILE * OWN :, lanes]))
    for copy in w2_loads:
        copy.wait()
    for g, tiles in enumerate(GROUPS):
        for t, fresh in update(tiles):
            for r in range(ROWS):
                state[t, r + 1, PAD : PAD + HALF] = fresh[HALF * r : HALF * (r + 1)]
                begin, end = fresh[HALF * r : HALF * r + 1], fresh[HALF * r + 63 : HALF * r + 64]
                e2d_out[t, r : r + 1] = jnp.where(row_is0, begin, end)
                e2p_out[t, r : r + 1] = jnp.where(row_is0, end, begin)
            z2_out[0, t] = fresh[HALF * 3 :].astype(b16)
            z2_out[1, t] = fresh[:HALF].astype(b16)
        when(has_n, z2[g][0].start)
        when(has_s, z2[g][1].start)
        when(has_far, e2[g][0].start)
        e2[g][1].start()

    for g, tiles in enumerate(GROUPS):
        sender = SENDERS[g]
        when(has_far, e2[sender][0].wait_recv)
        e2[sender][1].wait_recv()
        for t in tiles:
            edges(t, e2p_in[t], e2d_in[t])
        for d, there in ((0, has_s), (1, has_n)):
            @pl.when(there)
            def _(d=d, g=g, tiles=tiles):
                z2[g][d].wait_recv()
                for t in tiles:
                    state[t, 5 * d, PAD : PAD + HALF] = z2_in[d, t].astype(f32)
        propagate(tiles, g == 0, False)
    finish_sums()
    scale = 1.0 / (STEPS * STEPS * comps)
    packed = jnp.zeros((HALF, TILE), f32)
    for k in range(2):
        for r in range(ROWS):
            push = sums[2 + k, HALF * r : HALF * (r + 1), :].sum(axis=1, keepdims=True)
            packed = jnp.where(lane == 4 * k + r, scale * push, packed)
    small[...] = jnp.zeros_like(small)
    small[pl.ds(half_at, HALF), :] = packed
    small_t[...] = small[...].T
    st_out[...] = small_t[0:8]
    stress_pair.start()
    for n in range(4):
        lanes = slice(256 * n, 256 * (n + 1))
        activate(n, dot(p16[...], w1[:, lanes]))
    stress_pair.wait_recv()
    st_full[...] = st_out[...] + st_in[...]
    when(has_n, stress_n.start)
    when(has_s, stress_s.start)
    for g, tiles in enumerate(LAST_GROUPS):
        for t, fresh in update(tiles):
            if t >= OWN:
                f_out[mirror(t)] = fresh.astype(b16)
            if t <= OWN:
                for r in range(ROWS):
                    state[t, r + 1, PAD : PAD + HALF] = fresh[HALF * r : HALF * (r + 1)]
        if g < 3:
            final[g].start()

    sb_load.wait()
    when(has_s, stress_n.wait_recv)
    when(has_n, stress_s.wait_recv)
    for k in range(2):
        lines = [sz_in[0, 4 * k + 3 : 4 * k + 4]]
        lines += [st_full[4 * k + r : 4 * k + r + 1] for r in range(ROWS)]
        lines += [sz_in[1, 4 * k : 4 * k + 1]]
        for r in range(ROWS):
            total = sb[r, 0] * choose(srows, r, 0, *lines[r : r + 3])
            total = total + sb[r, 1] * choose(srows, r, 1, *lines[r : r + 3])
            stress = total.T.sum(axis=0, keepdims=True)
            wet = msk[r : r + 1, :].astype(f32)
            at = 16 * k
            o_out[at : at + 1, r, :] = o_out[at : at + 1, r, :] + wet * (STRESS_GAIN * stress)

    for g in range(3):
        final[g].wait_recv()
        for t in ((0, 1), (2, 3), (4,))[g]:
            for r in range(ROWS):
                own = state[t, r + 1, PAD : PAD + HALF]
                came = f_in[t, HALF * r : HALF * (r + 1)].astype(f32)
                turned = jnp.concatenate(
                    [jnp.where(half_is0, own, came), jnp.where(half_is0, came, own)], axis=0
                ).T
                if t < OWN:
                    out[pl.ds(me * HALF + TILE * t, TILE), r, :] = turned
                else:
                    out[pl.ds(other * (comps - HALF), HALF), r, :] = jnp.where(
                        half_is0, turned[:HALF], turned[HALF:]
                    )

    when(has_n, ocean_n.wait_send, z1_n.wait_send, zf_n.wait_send, stress_n.wait_send)
    when(has_s, ocean_s.wait_send, z1_s.wait_send, zf_s.wait_send, stress_s.wait_send)
    when(has_e, ocean_e.wait_send)
    when(has_w, ocean_w.wait_send)
    when(has_same, e_same.wait_send)
    when(has_far, e_diag.wait_send)
    for copy in swap + [e_pair, stress_pair] + final:
        copy.wait_send()
    for g in range(len(GROUPS)):
        when(has_n, z2[g][0].wait_send)
        when(has_s, z2[g][1].wait_send)
        when(has_far, e2[g][0].wait_send)
        e2[g][1].wait_send()


def kernel_call(
    spectra, first, second, table, ocean, wind, mask, cblocks, sblocks, crows, srows
):
    f32, b16 = jnp.float32, jnp.bfloat16
    comps = spectra.shape[0]
    units = first.shape[1]
    total = TILE * TILES
    shape = jax.ShapeDtypeStruct
    dma = pltpu.SemaphoreType.DMA
    groups = len(GROUPS)
    vmem = pltpu.VMEM
    scratch = [
        vmem((comps + 2 * HALF, ROWS, COLS), f32),
        vmem((total, units), b16),
        vmem((units, total), b16),
        vmem((TILES, 8, TILE), f32),
        vmem(ocean.shape, f32),
        vmem(wind.shape, f32),
        vmem(mask.shape, jnp.int32),
        vmem((ROWS, 2, HALF, COLS), f32),
        vmem((ROWS, 2, COLS, COLS), f32),
        vmem((TILES, ROWS + 2, HALF + 2 * PAD, TILE), f32),
        vmem((TILES, CELLS, TILE), f32),
        vmem((TILES, CELLS, TILE), f32),
        vmem((CELLS, total), b16),
        vmem((CELLS, units), f32),
        vmem((CELLS, units), b16),
        vmem((4, CELLS, TILE), f32),
        vmem((5, CELLS, TILE), f32),
        vmem((CELLS, TILE), f32),
        vmem((CELLS, TILE), f32),
        vmem((CELLS, TILE), f32),
        vmem((TILE, TILE), f32),
        vmem((TILE, TILE), f32),
        vmem((ROWS, OWN + 1, HALF, TILE), b16),
        vmem((ROWS, OWN + 1, HALF, TILE), b16),
        vmem((2, OWN + 1, HALF, TILE), b16),
        vmem((2, OWN + 1, HALF, TILE), b16),
        vmem((2, OWN + 1, HALF, TILE), b16),
        *[vmem((OWN + 1, 8, TILE), f32) for _ in range(7)],
        vmem((2, TILES, HALF, TILE), b16),
        vmem((2, TILES, HALF, TILE), b16),
        *[vmem((TILES, 8, TILE), f32) for _ in range(4)],
        vmem((2, 64, COLS), f32),
        vmem((2, 64, COLS), f32),
        vmem((256, COLS), f32),
        vmem((COLS, 256), f32),
        vmem((2, COLS, 256), f32),
        vmem((8, COLS), f32),
        vmem((8, COLS), f32),
        vmem((8, COLS), f32),
        vmem((2, 8, COLS), f32),
        vmem((OWN + 1, CELLS, TILE), b16),
        vmem((OWN + 1, CELLS, TILE), b16),
        dma((13,)),
        dma((2,)), dma((2,)),
        dma((2,)), dma((2,)),
        dma((ROWS,)), dma((ROWS,)),
        dma((2,)), dma((2,)),
        dma((2,)), dma((2,)),
        dma((3,)), dma((3,)),
        dma((2, groups)), dma((2, groups)),
        dma((2, groups)), dma((2, groups)),
        dma((3,)), dma((3,)),
        dma((3,)), dma((3,)),
    ]
    return pl.pallas_call(
        kernel,
        out_shape=(shape(spectra.shape, f32), shape(ocean.shape, f32)),
        in_specs=[pl.BlockSpec(memory_space=pl.ANY)] * 9
        + [pl.BlockSpec(memory_space=pltpu.SMEM)] * 2,
        out_specs=(pl.BlockSpec(memory_space=pltpu.VMEM),) * 2,
        scratch_shapes=scratch,
        compiler_params=pltpu.CompilerParams(
            vmem_limit_bytes=VMEM_LIMIT, collective_id=0, has_side_effects=True
        ),
    )(spectra, first, second, table, ocean, wind, mask, cblocks, sblocks, crows, srows)


def local_step(
    spectra,
    wind_field,
    sea_mask,
    first_layer,
    second_layer,
    ocean_state,
    current_blocks,
    current_rows,
    stress_blocks,
    stress_rows,
):
    half_freqs, directions, rows, cols = spectra.shape
    variables, levels = ocean_state.shape[:2]
    table = jnp.asarray(tables(2 * half_freqs, directions))
    state, ocean = kernel_call(
        spectra.reshape(half_freqs * directions, rows, cols),
        first_layer,
        second_layer,
        table,
        ocean_state.reshape(variables * levels, rows, cols),
        wind_field,
        sea_mask,
        current_blocks,
        stress_blocks,
        current_rows,
        stress_rows,
    )
    return state.reshape(spectra.shape), ocean.reshape(ocean_state.shape)


def solution(mesh):
    placed = (
        P("comp", None, "gy", "gx"),
        P(None, "gy", "gx"),
        P("gy", "gx"),
        P(),
        P(),
        P(None, None, "gy", "gx"),
        P("gy", None, "gx", None),
        P("gy", None, "gx"),
        P("gy", None, "gx", None),
        P("gy", None, "gx"),
    )
    return jax.shard_map(
        local_step,
        mesh=mesh,
        in_specs=placed,
        out_specs=(P("comp", None, "gy", "gx"), P(None, None, "gy", "gx")),
        check_vma=False,
    )
```

```python
import numpy as np

import jax
import jax.numpy as jnp
from jax import lax
from jax.experimental import pallas as pl
from jax.experimental.pallas import tpu as pltpu
from jax.sharding import PartitionSpec as P

CURRENT_GAIN = 0.08
WIND_GAIN = 0.06
DECAY_GAIN = 0.03
NONLINEAR_GAIN = 0.3
THERMAL = 0.2
HALINE = 0.8
CORIOLIS = 0.1
PRESSURE_GAIN = 0.2
LATERAL_MIX = 0.1
VERTICAL_MIX = 0.2
ADVECTION = 0.3
STRESS_GAIN = 150.0

STEPS = 2
ROWS = 4
COLS = 128
HALF = 64
CELLS = ROWS * HALF
TILE = 128
TILES = 9
OWN = 4
PAD = 8
GROUPS = ((0, 1), (5, 6), (4,), (2, 3), (7, 8))
SENDERS = (1, 0, 2, 4, 3)
LAST_GROUPS = ((4,), (5, 6), (7, 8), (0, 1), (2, 3))
ORDER = (1, 2, 0, 3)
SWAPPED = ((3, 0), (1, 2))
FINAL = (((0, 5), (5, 9)), ((0, 5), (5, 7), (7, 9)))
VMEM_LIMIT = 32 * 1024 * 1024


def tables(total, directions):
    index = np.arange(total, dtype=np.float64)
    group = 0.4 * np.exp(-3.0 * index / (total - 1))
    ratio = np.exp(2.0 * index / (total - 1) - 1.0)
    angles = 2.0 * np.pi * np.arange(directions) / directions
    cosines, sines = np.cos(angles), np.sin(angles)
    full = np.zeros((8, total, directions))
    full[0] = group[:, None] * cosines
    full[1] = group[:, None] * sines
    full[2] = cosines
    full[3] = sines
    full[4] = WIND_GAIN * 4.0 * group[:, None]
    full[5] = ratio[:, None]
    tiled = full.reshape(8, TILES, TILE).transpose(1, 0, 2)
    swapped = np.concatenate([tiled[5:], tiled[4:5], tiled[:4]])
    return np.stack([tiled, swapped]).astype(np.float32)


def mirror(t):
    return 4 if t == 4 else (t + 5) % 10


def kernel(
    spectra, first, second, table, ocean, wind, mask, cblocks, sblocks, crows_in, srows_in,
    out, o_out,
    spec, w1, w2, tab, oc, wnd, msk, cb, sb,
    state, prop, rate, p16, part, hidden, sums, cells, gain, back, squared, small, small_t,
    y_out, y_in, z1_out, z1_in, zf_in, es_out, es_in, ed_out, ed_in, ep_out, ep_in, el,
    z2_out, z2_in, e2d_out, e2d_in, e2p_out, e2p_in,
    oz_out, oz_in, ocat, ox_out, ox_in, st_out, st_in, st_full, sz_in, f_out, f_in, done,
    crows, srows, load, oz_send, oz_recv, ox_send, ox_recv, y_send, y_recv, z1_send, z1_recv,
    zf_send, zf_recv, e1_send, e1_recv, z2_send, z2_recv, e2_send, e2_recv,
    s_send, s_recv, f_send, f_recv,
):
    f32, b16 = jnp.float32, jnp.bfloat16
    me = lax.axis_index("comp")
    other = 1 - me
    gy, ny = lax.axis_index("gy"), lax.axis_size("gy")
    gx, nx = lax.axis_index("gx"), lax.axis_size("gx")
    comps = spectra.shape[0]
    mesh_ids = pl.DeviceIdType.MESH

    def local(source, target, n):
        return pltpu.make_async_copy(source, target, load.at[n])

    own_at = pl.multiple_of(me * 5 * TILE, TILE)
    far_at = pl.multiple_of(other * 5 * TILE, TILE)
    half_at = pl.multiple_of(me * HALF, HALF)
    spec_load = local(spectra, spec.at[pl.ds(HALF, comps)], 0)
    ocean_load = local(ocean, oc, 1)
    wind_load = local(wind, wnd, 2)
    mask_load = local(mask, msk, 3)
    table_load = local(table.at[me], tab, 4)
    cb_load = local(cblocks.at[:, :, pl.ds(half_at, HALF), :], cb, 5)
    sb_load = local(sblocks, sb, 6)
    w1_loads = [
        local(first.at[pl.ds(own_at, 512)], w1.at[pl.ds(0, 512)], 7),
        local(first.at[pl.ds(512, 128)], w1.at[pl.ds(512, 128)], 8),
        local(first.at[pl.ds(far_at, 512)], w1.at[pl.ds(640, 512)], 9),
    ]
    w2_loads = [
        local(second.at[:, pl.ds(own_at, 512)], w2.at[:, pl.ds(0, 512)], 10),
        local(second.at[:, pl.ds(512, 128)], w2.at[:, pl.ds(512, 128)], 11),
        local(second.at[:, pl.ds(far_at, 512)], w2.at[:, pl.ds(640, 512)], 12),
    ]
    crows_load = local(crows_in, crows, 13)
    srows_load = local(srows_in, srows, 14)
    for copy in (spec_load, ocean_load, wind_load, mask_load, table_load, crows_load):
        copy.start()

    for ref in (es_in, ed_in, e2d_in, sz_in, ox_in, oz_in):
        ref[...] = jnp.zeros_like(ref)

    has_s, has_n = gy > 0, gy < ny - 1
    has_w, has_e = gx > 0, gx < nx - 1
    south = {"gy": lax.rem(gy + ny - 1, ny)}
    north = {"gy": lax.rem(gy + 1, ny)}
    west = {"gx": lax.rem(gx + nx - 1, nx)}
    east = {"gx": lax.rem(gx + 1, nx)}
    pair = {"comp": other}
    far_gx = gx + 2 * me - 1
    has_far = jnp.logical_and(far_gx >= 0, far_gx < nx)
    diag = {"comp": other, "gx": lax.rem(far_gx + nx, nx)}
    same_gx = gx + 1 - 2 * me
    has_same = jnp.logical_and(same_gx >= 0, same_gx < nx)
    same = {"gx": lax.rem(same_gx + nx, nx)}

    barrier = pltpu.get_barrier_semaphore()
    greet = ((has_s, south), (has_n, north), (has_w, west), (has_e, east), (has_far, diag))
    for there, place in greet:
        @pl.when(there)
        def _(place=place):
            pl.semaphore_signal(barrier, inc=1, device_id=place, device_id_type=mesh_ids)
    pl.semaphore_signal(barrier, inc=1, device_id=pair, device_id_type=mesh_ids)

    def remote(source, target, send, recv, where):
        return pltpu.make_async_remote_copy(
            src_ref=source, dst_ref=target, send_sem=send, recv_sem=recv,
            device_id=where, device_id_type=mesh_ids,
        )

    ocean_n = remote(oz_out.at[0], oz_in.at[0], oz_send.at[0], oz_recv.at[0], north)
    ocean_s = remote(oz_out.at[1], oz_in.at[1], oz_send.at[1], oz_recv.at[1], south)
    ocean_e = remote(
        ox_out.at[pl.ds(120, 8)], ox_in.at[0, pl.ds(120, 8)], ox_send.at[0], ox_recv.at[0], east
    )
    ocean_w = remote(
        ox_out.at[pl.ds(0, 8)], ox_in.at[1, pl.ds(0, 8)], ox_send.at[1], ox_recv.at[1], west
    )
    swap = [
        [
            remote(
                y_out.at[p, part_of], y_in.at[p, part_of], y_send.at[p, n], y_recv.at[p, n], pair
            )
            for n, part_of in enumerate((pl.ds(0, 4), pl.ds(4, 5)))
        ]
        for p in range(2)
    ]
    z1_n = remote(z1_out.at[0], z1_in.at[0], z1_send.at[0], z1_recv.at[0], north)
    z1_s = remote(z1_out.at[1], z1_in.at[1], z1_send.at[1], z1_recv.at[1], south)
    zf_n = remote(y_in.at[0, pl.ds(0, 5)], zf_in.at[0], zf_send.at[0], zf_recv.at[0], north)
    zf_s = remote(y_in.at[0, pl.ds(4, 5)], zf_in.at[1], zf_send.at[1], zf_recv.at[1], south)
    e_same = remote(es_out, es_in, e1_send.at[0], e1_recv.at[0], same)
    e_diag = remote(ed_out, ed_in, e1_send.at[1], e1_recv.at[1], diag)
    e_pair = remote(ep_out, ep_in, e1_send.at[2], e1_recv.at[2], pair)

    def span(tiles):
        return pl.ds(tiles[0], len(tiles))

    z2 = []
    e2 = []
    for g, tiles in enumerate(GROUPS):
        part_of = span(tiles)
        z2.append([
            remote(
                z2_out.at[d, part_of], z2_in.at[d, part_of],
                z2_send.at[d, g], z2_recv.at[d, g], (north, south)[d],
            )
            for d in range(2)
        ])
        there = SENDERS[g]
        e2.append([
            remote(e2d_out.at[g], e2d_in.at[there], e2_send.at[0, g], e2_recv.at[0, g], diag),
            remote(e2p_out.at[g], e2p_in.at[there], e2_send.at[1, g], e2_recv.at[1, g], pair),
        ])
    stress_pair = remote(st_out, st_in, s_send.at[0], s_recv.at[0], pair)
    stress_n = remote(st_full, sz_in.at[0], s_send.at[1], s_recv.at[1], north)
    stress_s = remote(st_full, sz_in.at[1], s_send.at[2], s_recv.at[2], south)
    final = []
    for h in range(2):
        final.append([])
        for n, (begin, end) in enumerate(FINAL[h]):
            slots = pl.ds(begin, end - begin)
            final[h].append(
                remote(
                    f_out.at[h, slots], f_in.at[h, slots], f_send.at[h, n], f_recv.at[h, n], pair
                )
            )

    def when(condition, *actions):
        @pl.when(condition)
        def _():
            for action in actions:
                action()

    for edge in (0, ROWS + 1):
        state[:, edge, PAD : PAD + HALF] = jnp.zeros((TILES, HALF, TILE), f32)
    spec[:HALF] = jnp.zeros((HALF, ROWS, COLS), f32)
    spec[HALF + comps :] = jnp.zeros((HALF, ROWS, COLS), f32)

    half_is0 = jnp.broadcast_to(me, (HALF, TILE)) == 0
    row_is0 = jnp.broadcast_to(me, (1, TILE)) == 0
    lane = lax.broadcasted_iota(jnp.int32, (HALF, TILE), 1)
    mine = jnp.where(lane < 64, 0, 1) == me

    def pack(first_row, second_row, low_lanes):
        left = jnp.where(low_lanes, first_row, pltpu.roll(first_row, 64, 1))
        right = jnp.where(low_lanes, pltpu.roll(second_row, 64, 1), second_row)
        return jnp.where(lane < 64, left, right).astype(b16)

    def unpack(packed, side, low_lanes):
        wide = packed.astype(f32)
        turned = pltpu.roll(wide, 64, 1)
        if side == 0:
            return jnp.where(low_lanes, wide, turned)
        return jnp.where(low_lanes, turned, wide)

    is_low, is_high = half_is0, jnp.logical_not(half_is0)
    starts = [HALF + me * HALF + TILE * t for t in range(OWN)] + [other * (comps + HALF - 64)]
    spec_load.wait()
    for copy in [cb_load] + w1_loads + w2_loads + [sb_load, srows_load]:
        copy.start()
    counted = [jnp.where(there, 1, 0) for there, _ in greet]
    for p, pair_rows in enumerate(SWAPPED):
        kept = []
        for side, r in enumerate(pair_rows):
            for t in range(OWN + 1):
                turned = spec[pl.ds(starts[t], TILE), r, :].T
                low, high = turned[:HALF], turned[HALF:]
                own = jnp.where(half_is0, low, high)
                far = jnp.where(half_is0, high, low)
                state[t, r + 1, PAD : PAD + HALF] = own
                if t < OWN:
                    y_out[p, 5 * side + t] = far.astype(b16)
                else:
                    kept.append(far)
                if r == 3:
                    z1_out[0, t] = own.astype(b16)
                if r == 0:
                    z1_out[1, t] = own.astype(b16)
                at = 4 * t + r
                es_out[at : at + 1] = jnp.where(row_is0, turned[127:128], turned[0:1])
                ed_out[at : at + 1] = jnp.where(row_is0, turned[0:1], turned[127:128])
                ep_out[at : at + 1] = jnp.where(row_is0, turned[63:64], turned[64:65])
                el[at : at + 1] = jnp.where(row_is0, turned[64:65], turned[63:64])
            if r == 3:
                pl.semaphore_wait(barrier, 1 + sum(counted))
            if side == 0:
                swap[p][0].start()
            if r == 3:
                when(has_n, z1_n.start)
            if r == 0:
                when(has_s, z1_s.start)
        y_out[p, 4] = pack(kept[0], kept[1], is_low)
        swap[p][1].start()
    when(has_same, e_same.start)
    when(has_far, e_diag.start)
    e_pair.start()

    ocean_load.wait()
    oz_out[0] = oc[:, ROWS - 1, :]
    oz_out[1] = oc[:, 0, :]
    when(has_n, ocean_n.start)
    when(has_s, ocean_s.start)
    for r in range(ROWS):
        ocat[64 * r : 64 * (r + 1), :] = oc[:, r, :]
    ox_out[...] = ocat[...].T
    when(has_e, ocean_e.start)
    when(has_w, ocean_w.start)

    wind_load.wait()
    mask_load.wait()
    table_load.wait()
    small[...] = jnp.zeros_like(small)
    small[0:4] = msk[...].astype(f32)
    small[4:8] = WIND_GAIN * wnd[0]
    small[8:12] = WIND_GAIN * wnd[1]
    small_t[...] = small[...].T
    columns = small_t[pl.ds(half_at, HALF), :]
    for q in range(3):
        for r in range(ROWS):
            n = 4 * q + r
            at = HALF * ORDER.index(r)
            cells[2 + q, at : at + HALF, :] = jnp.broadcast_to(
                columns[:, n : n + 1], (HALF, TILE)
            )
    cb_load.wait()
    crows_load.wait()
    when(has_s, ocean_n.wait_recv)
    when(has_n, ocean_s.wait_recv)

    def choose(rows_ref, r, b, below, here, above):
        offset = jnp.broadcast_to(rows_ref[b, 0, r] - gy * ROWS - r, (1, COLS))
        return jnp.where(offset < 0, below, jnp.where(offset == 0, here, above))

    for k in range(2):
        at = 16 * k
        lines = [oz_in[0, at : at + 1]]
        lines += [oc[at : at + 1, r, :] for r in range(ROWS)]
        lines += [oz_in[1, at : at + 1]]
        for r in range(ROWS):
            total = cb[r, 0] * choose(crows, r, 0, *lines[r : r + 3])
            total = total + cb[r, 1] * choose(crows, r, 1, *lines[r : r + 3])
            place = HALF * ORDER.index(r)
            cells[k, place : place + HALF, :] = jnp.broadcast_to(
                CURRENT_GAIN * total.sum(axis=1, keepdims=True), (HALF, TILE)
            )

    def edges(t, pair_side, far_side):
        for r in range(ROWS):
            near, far = pair_side[r : r + 1], far_side[r : r + 1]
            state[t, r + 1, PAD - 1 : PAD] = jnp.where(row_is0, far, near)
            state[t, r + 1, PAD + HALF : PAD + HALF + 1] = jnp.where(row_is0, near, far)

    def propagate(tiles, h, fresh, fresh_push):
        def body(i, carry):
            at = pl.multiple_of((2 * h + i) * HALF, HALF)
            r = 3 * i if h else 1 + i
            for lo in (0, 32):
                cell = pl.ds(at + lo, 32)
                cur_x, cur_y, wet, wind_x, wind_y = (cells[q, cell, :] for q in range(5))
                zero = jnp.zeros((32, TILE), f32)
                totals = [
                    zero if (fresh if q < 2 else fresh_push) else sums[q, cell, :]
                    for q in range(4)
                ]
                for t in tiles:
                    speed_x, speed_y, cos, sin, phase, ratio = (
                        tab[t, q : q + 1, :] for q in range(6)
                    )
                    top = PAD + lo
                    here = state[t, r + 1, top : top + 32]
                    before = state[t, r + 1, top - 1 : top + 31]
                    after = state[t, r + 1, top + 1 : top + 33]
                    below = state[t, r, top : top + 32]
                    above = state[t, r + 2, top : top + 32]
                    cx = speed_x + cur_x
                    cy = speed_y + cur_y
                    flux = jnp.abs(cx) * (here - jnp.where(cx > 0.0, before, after))
                    flux = flux + jnp.abs(cy) * (here - jnp.where(cy > 0.0, below, above))
                    moved = wet * (here - flux)
                    growth = jnp.maximum(wind_x * cos + wind_y * sin - phase, 0.0)
                    pushed = growth * moved
                    prop[t, cell, :] = moved
                    rate[t, cell, :] = growth
                    p16[cell, TILE * t : TILE * (t + 1)] = moved.astype(b16)
                    parts = (moved, ratio * moved, pushed * cos, pushed * sin)
                    totals = [a + b for a, b in zip(totals, parts)]
                for q in range(4):
                    sums[q, cell, :] = totals[q]
            return carry

        lax.fori_loop(0, 2, body, 0)

    def finish_sums(rows):
        total = STEPS * comps
        count = rows.stop - rows.start

        def spread(n):
            return jnp.broadcast_to(
                sums[n, rows, :].sum(axis=1, keepdims=True), (count, TILE)
            )

        floor = jnp.maximum(spread(0), 1.0)
        share = spread(1) / floor
        squared[rows] = DECAY_GAIN * share * share
        gain[rows] = (0.5 * total) / floor
        back[rows] = (NONLINEAR_GAIN / total) * floor

    def dot(left, right):
        return lax.dot_general(
            left, right, (((1,), (0,)), ((), ())), preferred_element_type=f32
        )

    def activate(n, pre, rows):
        for j in range(2):
            half = pre[:, TILE * j : TILE * (j + 1)] * gain[rows]
            at = 256 * n + TILE * j
            hidden[rows, at : at + TILE] = (half + half * jnp.tanh(half)).astype(b16)

    def update(tiles, rows):
        at = TILE * tiles[0]
        moved = dot(hidden[rows], w2[:, at : at + TILE * len(tiles)])
        for j, t in enumerate(tiles):
            transfer = moved[:, TILE * j : TILE * (j + 1)].astype(b16).astype(f32)
            fresh = prop[t, rows] * jnp.exp(rate[t, rows] - tab[t, 5:6, :] * squared[rows])
            yield j, t, fresh + back[rows] * transfer

    whole = slice(0, CELLS)
    halves = (slice(0, CELLS // 2), slice(CELLS // 2, CELLS))

    when(has_s, z1_n.wait_recv)
    when(has_n, z1_s.wait_recv)
    when(has_far, e_same.wait_recv)
    for t in range(OWN):
        edges(t, el[4 * t : 4 * t + 4], es_in[4 * t : 4 * t + 4])
    for d, there in ((0, has_s), (1, has_n)):
        @pl.when(there)
        def _(d=d):
            for t in range(OWN):
                state[t, 5 * d, PAD : PAD + HALF] = z1_in[d, t].astype(f32)
    for h in range(2):
        propagate(range(OWN), h, True, True)
    swap[0][0].wait_recv()
    swap[0][1].wait_recv()
    when(has_n, zf_n.start)
    when(has_s, zf_s.start)
    for copy in w1_loads:
        copy.wait()
    for n in range(4):
        lanes = slice(256 * n, 256 * (n + 1))
        part[:, lanes] = dot(p16[:, : TILE * OWN], w1[: TILE * OWN, lanes])

    when(has_w, ocean_e.wait_recv)
    when(has_e, ocean_w.wait_recv)
    from_w, from_e = ox_in[0].T, ox_in[1].T
    lane64 = lax.broadcasted_iota(jnp.int32, (64, COLS), 1)
    level64 = lax.rem(lax.broadcasted_iota(jnp.int32, (64, COLS), 0), 16)
    level = lax.broadcasted_iota(jnp.int32, (16, COLS), 0)

    def density(field):
        return HALINE * field[48:64] - THERMAL * field[32:48]

    def pressure(dense):
        running = dense
        for shift in (1, 2, 4, 8):
            running = running + jnp.where(level >= shift, pltpu.roll(running, shift, 0), 0.0)
        return running - 0.5 * dense

    for r in range(ROWS):
        here = oc[:, r, :]
        low = oz_in[0] if r == 0 else oc[:, r - 1, :]
        high = oz_in[1] if r == ROWS - 1 else oc[:, r + 1, :]
        lines = slice(64 * r, 64 * (r + 1))
        left = pltpu.roll(jnp.where(lane64 == COLS - 1, from_w[lines], here), 1, 1)
        right = pltpu.roll(jnp.where(lane64 == 0, from_e[lines], here), COLS - 1, 1)
        upper = jnp.where(level64 == 0, here, pltpu.roll(here, 1, 0))
        lower = jnp.where(level64 == 15, here, pltpu.roll(here, 63, 0))
        mixed = LATERAL_MIX * (left + right + low + high - 4.0 * here)
        mixed = mixed + VERTICAL_MIX * (upper + lower - 2.0 * here)
        across, along = right - left, high - low
        speed_u, speed_v = here[0:16], here[16:32]
        half_gain = 0.5 * PRESSURE_GAIN
        du = CORIOLIS * speed_v - half_gain * pressure(density(across))
        dv = -CORIOLIS * speed_u - half_gain * pressure(density(along))
        pull = -0.5 * ADVECTION
        dtemp = pull * (speed_u * across[32:48] + speed_v * along[32:48])
        dsalt = pull * (speed_u * across[48:64] + speed_v * along[48:64])
        tendency = mixed + jnp.concatenate([du, dv, dtemp, dsalt], axis=0)
        o_out[:, r, :] = here + msk[r : r + 1, :].astype(f32) * tendency

    for p, pair_rows in enumerate(SWAPPED):
        if p == 1:
            swap[1][0].wait_recv()
            swap[1][1].wait_recv()
        for side, r in enumerate(pair_rows):
            for t in range(OWN):
                state[5 + t, r + 1, PAD : PAD + HALF] = y_in[p, 5 * side + t].astype(f32)
            state[4, r + 1, PAD : PAD + HALF] = jnp.where(
                mine, state[4, r + 1, PAD : PAD + HALF], unpack(y_in[p, 4], side, is_high)
            )
    when(has_far, e_diag.wait_recv)
    e_pair.wait_recv()
    for t in range(OWN):
        lines = slice(4 * t, 4 * t + 4)
        edges(5 + t, ep_in[lines], ed_in[lines])
    edges(
        4,
        jnp.where(mine[:4], el[16:20], ep_in[16:20]),
        jnp.where(mine[:4], es_in[16:20], ed_in[16:20]),
    )
    for d, there, copy in ((0, has_s, zf_n), (1, has_n, zf_s)):
        @pl.when(there)
        def _(d=d, copy=copy):
            copy.wait_recv()
            for t in range(OWN):
                state[5 + t, 5 * d, PAD : PAD + HALF] = zf_in[d, t + d].astype(f32)
            state[4, 5 * d, PAD : PAD + HALF] = jnp.where(
                mine, z1_in[d, 4].astype(f32), unpack(zf_in[d, 4 - 4 * d], d, is_high)
            )
    for h in range(2):
        propagate(range(OWN, TILES), h, False, False)
    finish_sums(whole)
    for n in range(4):
        lanes = slice(256 * n, 256 * (n + 1))
        pre = part[:, lanes] + dot(p16[:, TILE * OWN :], w1[TILE * OWN :, lanes])
        activate(n, pre, whole)
    for copy in w2_loads:
        copy.wait()
    for g, tiles in enumerate(GROUPS):
        for j, t, fresh in update(tiles, whole):
            for n, r in enumerate(ORDER):
                block = fresh[HALF * n : HALF * (n + 1)]
                state[t, r + 1, PAD : PAD + HALF] = block
                begin, end = block[:1], block[HALF - 1 :]
                at = 4 * j + r
                e2d_out[g, at : at + 1] = jnp.where(row_is0, begin, end)
                e2p_out[g, at : at + 1] = jnp.where(row_is0, end, begin)
                if r == ROWS - 1:
                    z2_out[0, t] = block.astype(b16)
                if r == 0:
                    z2_out[1, t] = block.astype(b16)
        when(has_far, e2[g][0].start)
        e2[g][1].start()
        when(has_n, z2[g][0].start)
        when(has_s, z2[g][1].start)

    def last_updates(h):
        rows = halves[h]
        for tiles in LAST_GROUPS:
            for j, t, fresh in update(tiles, rows):
                upper, under = fresh[:HALF], fresh[HALF:]
                if t > OWN:
                    at = 1 + 2 * (t - 5)
                    f_out[h, at] = upper.astype(b16)
                    f_out[h, at + 1] = under.astype(b16)
                if t == OWN:
                    f_out[h, 0] = pack(upper, under, is_high)
                if t <= OWN:
                    done[t, rows] = fresh
            if tiles == (5, 6):
                final[h][0].start()
            if tiles == (7, 8):
                for copy in final[h][1:]:
                    copy.start()

    for g, tiles in enumerate(GROUPS):
        when(has_far, e2[SENDERS[g]][0].wait_recv)
        e2[SENDERS[g]][1].wait_recv()
        for j, t in enumerate(tiles):
            lines = slice(4 * j, 4 * j + 4)
            edges(t, e2p_in[g, lines], e2d_in[g, lines])
        propagate(tiles, 0, g == 0, False)
    finish_sums(halves[0])
    for n in range(4):
        lanes = slice(256 * n, 256 * (n + 1))
        activate(n, dot(p16[halves[0]], w1[:, lanes]), halves[0])
    last_updates(0)

    for g, tiles in enumerate(GROUPS):
        for d, there in ((0, has_s), (1, has_n)):
            @pl.when(there)
            def _(d=d, g=g, tiles=tiles):
                z2[g][d].wait_recv()
                for t in tiles:
                    state[t, 5 * d, PAD : PAD + HALF] = z2_in[d, t].astype(f32)
        propagate(tiles, 1, g == 0, False)
    finish_sums(halves[1])
    scale = 1.0 / (STEPS * STEPS * comps)
    packed = jnp.zeros((HALF, TILE), f32)
    for k in range(2):
        for n, r in enumerate(ORDER):
            push = sums[2 + k, HALF * n : HALF * (n + 1), :].sum(axis=1, keepdims=True)
            packed = jnp.where(lane == 4 * k + r, scale * push, packed)
    small[...] = jnp.zeros_like(small)
    small[pl.ds(half_at, HALF), :] = packed
    small_t[...] = small[...].T
    st_out[...] = small_t[0:8]
    stress_pair.start()
    for n in range(4):
        lanes = slice(256 * n, 256 * (n + 1))
        activate(n, dot(p16[halves[1]], w1[:, lanes]), halves[1])
    last_updates(1)
    stress_pair.wait_recv()
    st_full[...] = st_out[...] + st_in[...]
    when(has_n, stress_n.start)
    when(has_s, stress_s.start)

    def turn_back(h, t):
        for side in range(2):
            n = 2 * h + side
            own = done[t, HALF * n : HALF * (n + 1)]
            if t < OWN:
                came = f_in[h, 1 + 2 * t + side].astype(f32)
            else:
                came = unpack(f_in[h, 0], side, is_low)
            turned = jnp.concatenate(
                [jnp.where(half_is0, own, came), jnp.where(half_is0, came, own)], axis=0
            ).T
            r = ORDER[n]
            if t < OWN:
                out[pl.ds(me * HALF + TILE * t, TILE), r, :] = turned
            else:
                out[pl.ds(other * (comps - HALF), HALF), r, :] = jnp.where(
                    half_is0, turned[:HALF], turned[HALF:]
                )

    final[0][0].wait_recv()
    for t in (4, 0, 1):
        turn_back(0, t)
    final[0][1].wait_recv()
    for t in (2, 3):
        turn_back(0, t)

    sb_load.wait()
    srows_load.wait()
    when(has_s, stress_n.wait_recv)
    when(has_n, stress_s.wait_recv)
    for k in range(2):
        lines = [sz_in[0, 4 * k + 3 : 4 * k + 4]]
        lines += [st_full[4 * k + r : 4 * k + r + 1] for r in range(ROWS)]
        lines += [sz_in[1, 4 * k : 4 * k + 1]]
        for r in range(ROWS):
            total = sb[r, 0] * choose(srows, r, 0, *lines[r : r + 3])
            total = total + sb[r, 1] * choose(srows, r, 1, *lines[r : r + 3])
            stress = total.T.sum(axis=0, keepdims=True)
            wet = msk[r : r + 1, :].astype(f32)
            at = 16 * k
            o_out[at : at + 1, r, :] = o_out[at : at + 1, r, :] + wet * (STRESS_GAIN * stress)

    for n, tiles in enumerate(((4, 0, 1), (2,), (3,))):
        final[1][n].wait_recv()
        for t in tiles:
            turn_back(1, t)

    when(has_n, ocean_n.wait_send, z1_n.wait_send, zf_n.wait_send, stress_n.wait_send)
    when(has_s, ocean_s.wait_send, z1_s.wait_send, zf_s.wait_send, stress_s.wait_send)
    when(has_e, ocean_e.wait_send)
    when(has_w, ocean_w.wait_send)
    when(has_same, e_same.wait_send)
    when(has_far, e_diag.wait_send)
    for copy in swap[0] + swap[1] + [e_pair, stress_pair] + final[0] + final[1]:
        copy.wait_send()
    for g in range(len(GROUPS)):
        when(has_n, z2[g][0].wait_send)
        when(has_s, z2[g][1].wait_send)
        when(has_far, e2[g][0].wait_send)
        e2[g][1].wait_send()


def kernel_call(
    spectra, first, second, table, ocean, wind, mask, cblocks, sblocks, crows, srows
):
    f32, b16 = jnp.float32, jnp.bfloat16
    comps = spectra.shape[0]
    units = first.shape[1]
    total = TILE * TILES
    shape = jax.ShapeDtypeStruct
    dma = pltpu.SemaphoreType.DMA
    groups = len(GROUPS)
    vmem = pltpu.VMEM
    scratch = [
        vmem((comps + 2 * HALF, ROWS, COLS), f32),
        vmem((total, units), b16),
        vmem((units, total), b16),
        vmem((TILES, 8, TILE), f32),
        vmem(ocean.shape, f32),
        vmem(wind.shape, f32),
        vmem(mask.shape, jnp.int32),
        vmem((ROWS, 2, HALF, COLS), f32),
        vmem((ROWS, 2, COLS, COLS), f32),
        vmem((TILES, ROWS + 2, HALF + 2 * PAD, TILE), f32),
        vmem((TILES, CELLS, TILE), f32),
        vmem((TILES, CELLS, TILE), f32),
        vmem((CELLS, total), b16),
        vmem((CELLS, units), f32),
        vmem((CELLS, units), b16),
        vmem((4, CELLS, TILE), f32),
        vmem((5, CELLS, TILE), f32),
        vmem((CELLS, TILE), f32),
        vmem((CELLS, TILE), f32),
        vmem((CELLS, TILE), f32),
        vmem((TILE, TILE), f32),
        vmem((TILE, TILE), f32),
        vmem((2, TILES, HALF, TILE), b16),
        vmem((2, TILES, HALF, TILE), b16),
        vmem((2, OWN + 1, HALF, TILE), b16),
        vmem((2, OWN + 1, HALF, TILE), b16),
        vmem((2, OWN + 1, HALF, TILE), b16),
        *[vmem((24, TILE), f32) for _ in range(7)],
        vmem((2, TILES, HALF, TILE), b16),
        vmem((2, TILES, HALF, TILE), b16),
        *[vmem((groups, 8, TILE), f32) for _ in range(4)],
        vmem((2, 64, COLS), f32),
        vmem((2, 64, COLS), f32),
        vmem((256, COLS), f32),
        vmem((COLS, 256), f32),
        vmem((2, COLS, 256), f32),
        vmem((8, COLS), f32),
        vmem((8, COLS), f32),
        vmem((8, COLS), f32),
        vmem((2, 8, COLS), f32),
        vmem((2, TILES, HALF, TILE), b16),
        vmem((2, TILES, HALF, TILE), b16),
        vmem((OWN + 1, CELLS, TILE), f32),
        pltpu.SMEM((2, 1, ROWS), jnp.int32),
        pltpu.SMEM((2, 1, ROWS), jnp.int32),
        dma((15,)),
        dma((2,)), dma((2,)),
        dma((2,)), dma((2,)),
        dma((2, 2)), dma((2, 2)),
        dma((2,)), dma((2,)),
        dma((2,)), dma((2,)),
        dma((3,)), dma((3,)),
        dma((2, groups)), dma((2, groups)),
        dma((2, groups)), dma((2, groups)),
        dma((3,)), dma((3,)),
        dma((2, 3)), dma((2, 3)),
    ]
    return pl.pallas_call(
        kernel,
        out_shape=(shape(spectra.shape, f32), shape(ocean.shape, f32)),
        in_specs=[pl.BlockSpec(memory_space=pl.ANY)] * 11,
        out_specs=(pl.BlockSpec(memory_space=pltpu.VMEM),) * 2,
        scratch_shapes=scratch,
        compiler_params=pltpu.CompilerParams(
            vmem_limit_bytes=VMEM_LIMIT, collective_id=0, has_side_effects=True
        ),
    )(*(
        pltpu.with_memory_space_constraint(x, pltpu.HBM)
        for x in (
            spectra, first, second, table, ocean, wind, mask, cblocks, sblocks, crows, srows
        )
    ))


PIECES = 4


def place_kernel(a, b, a_out, b_out, sems):
    rows = a.shape[0] // PIECES
    copies = [pltpu.make_async_copy(b, b_out, sems.at[PIECES])]
    for n in range(PIECES):
        part = pl.ds(n * rows, rows)
        copies.append(pltpu.make_async_copy(a.at[part], a_out.at[part], sems.at[n]))
    for copy in copies:
        copy.start()
    for copy in copies:
        copy.wait()


def place_call(a, b):
    shape = jax.ShapeDtypeStruct
    return pl.pallas_call(
        place_kernel,
        out_shape=(shape(a.shape, a.dtype), shape(b.shape, b.dtype)),
        in_specs=[pl.BlockSpec(memory_space=pl.ANY)] * 2,
        out_specs=(pl.BlockSpec(memory_space=pl.ANY),) * 2,
        scratch_shapes=[pltpu.SemaphoreType.DMA((PIECES + 1,))],
        compiler_params=pltpu.CompilerParams(vmem_limit_bytes=VMEM_LIMIT),
    )(a, b)


def local_step(
    spectra,
    wind_field,
    sea_mask,
    first_layer,
    second_layer,
    ocean_state,
    current_blocks,
    current_rows,
    stress_blocks,
    stress_rows,
):
    half_freqs, directions, rows, cols = spectra.shape
    variables, levels = ocean_state.shape[:2]
    table = jnp.asarray(tables(2 * half_freqs, directions))
    state, ocean = kernel_call(
        spectra.reshape(half_freqs * directions, rows, cols),
        first_layer,
        second_layer,
        table,
        ocean_state.reshape(variables * levels, rows, cols),
        wind_field,
        sea_mask,
        current_blocks,
        stress_blocks,
        current_rows.transpose(1, 2, 0),
        stress_rows.transpose(1, 2, 0),
    )
    state, ocean = place_call(state, ocean)
    return state.reshape(spectra.shape), ocean.reshape(ocean_state.shape)


def solution(mesh):
    placed = (
        P("comp", None, "gy", "gx"),
        P(None, "gy", "gx"),
        P("gy", "gx"),
        P(),
        P(),
        P(None, None, "gy", "gx"),
        P("gy", None, "gx", None),
        P("gy", None, "gx"),
        P("gy", None, "gx", None),
        P("gy", None, "gx"),
    )
    return jax.shard_map(
        local_step,
        mesh=mesh,
        in_specs=placed,
        out_specs=(P("comp", None, "gy", "gx"), P(None, None, "gy", "gx")),
        check_vma=False,
    )
```

```python
import numpy as np

import jax
import jax.numpy as jnp
from jax import lax
from jax.experimental import pallas as pl
from jax.experimental.pallas import tpu as pltpu
from jax.sharding import PartitionSpec as P

CURRENT_GAIN = 0.08
WIND_GAIN = 0.06
DECAY_GAIN = 0.03
NONLINEAR_GAIN = 0.3
THERMAL = 0.2
HALINE = 0.8
CORIOLIS = 0.1
PRESSURE_GAIN = 0.2
LATERAL_MIX = 0.1
VERTICAL_MIX = 0.2
ADVECTION = 0.3
STRESS_GAIN = 150.0

STEPS = 2
ROWS = 4
COLS = 128
HALF = 64
CELLS = ROWS * HALF
TILE = 128
TILES = 9
OWN = 4
PAD = 8
GROUPS = ((0, 1, 5, 6), (2, 3, 7, 8, 4))
PLACED = GROUPS[0] + GROUPS[1]
PRODUCTS = (((0, 1), (5, 6)), ((2, 3), (7, 8), (4,)))
SWAP_SLOTS = (
    (pl.ds(0, 2), pl.ds(7, 2), pl.ds(2, 3), pl.ds(5, 2)),
    (pl.ds(0, 5), pl.ds(5, 4)),
)
NORTH_SLOTS = ((pl.ds(0, 2), pl.ds(0, 2)), (pl.ds(2, 3), pl.ds(2, 3)))
SOUTH_SLOTS = ((pl.ds(7, 2), pl.ds(3, 2)), (pl.ds(4, 3), pl.ds(0, 3)))
ORDER = (1, 2, 0, 3)
SWAPPED = ((3, 0), (1, 2))
FINAL = (((0, 4), (4, 9)), ((0, 4), (4, 8), (8, 9)))
VMEM_LIMIT = 32 * 1024 * 1024


def tables(total, directions):
    index = np.arange(total, dtype=np.float64)
    group = 0.4 * np.exp(-3.0 * index / (total - 1))
    ratio = np.exp(2.0 * index / (total - 1) - 1.0)
    angles = 2.0 * np.pi * np.arange(directions) / directions
    cosines, sines = np.cos(angles), np.sin(angles)
    full = np.zeros((8, total, directions))
    full[0] = group[:, None] * cosines
    full[1] = group[:, None] * sines
    full[2] = cosines
    full[3] = sines
    full[4] = WIND_GAIN * 4.0 * group[:, None]
    full[5] = ratio[:, None]
    tiled = full.reshape(8, TILES, TILE).transpose(1, 0, 2)
    swapped = np.concatenate([tiled[5:], tiled[4:5], tiled[:4]])
    return np.stack([tiled, swapped]).astype(np.float32)


def mirror(t):
    return 4 if t == 4 else (t + 5) % 10


def kernel(
    spectra, first, second, table, ocean, wind, mask, cblocks, sblocks, crows_in, srows_in,
    out, o_out,
    spec, w1, w2, tab, oc, wnd, msk, cb, sb,
    state, prop, rate, p16, part, hidden, sums, cells, gain, back, squared, small, small_t,
    y_out, y_in, z1_out, z1_in, zf_in, es_out, es_in, ed_out, ed_in, ep_out, ep_in, el,
    z2_out, z2_in, e2d_out, e2d_in, e2p_out, e2p_in,
    oz_out, oz_in, ocat, ox_out, ox_in, st_out, st_in, st_full, sz_in, sx_in, f_out, f_in, done,
    crows, srows, load, oz_send, oz_recv, ox_send, ox_recv, y_send, y_recv, z1_send, z1_recv,
    zf_send, zf_recv, e1_send, e1_recv, z2_send, z2_recv, e2_send, e2_recv,
    s_send, s_recv, f_send, f_recv,
):
    f32, b16 = jnp.float32, jnp.bfloat16
    me = lax.axis_index("comp")
    other = 1 - me
    gy, ny = lax.axis_index("gy"), lax.axis_size("gy")
    gx, nx = lax.axis_index("gx"), lax.axis_size("gx")
    comps = spectra.shape[0]
    mesh_ids = pl.DeviceIdType.MESH

    def local(source, target, n):
        return pltpu.make_async_copy(source, target, load.at[n])

    own_at = pl.multiple_of(me * 5 * TILE, TILE)
    far_at = pl.multiple_of(other * 5 * TILE, TILE)
    half_at = pl.multiple_of(me * HALF, HALF)
    spec_load = local(spectra, spec.at[pl.ds(HALF, comps)], 0)
    ocean_load = local(ocean, oc, 1)
    wind_load = local(wind, wnd, 2)
    mask_load = local(mask, msk, 3)
    table_load = local(table.at[me], tab, 4)
    cb_load = local(cblocks.at[:, :, pl.ds(half_at, HALF), :], cb, 5)
    sb_load = local(sblocks, sb, 6)
    w1_loads = [
        local(first.at[pl.ds(own_at, 512)], w1.at[pl.ds(0, 512)], 7),
        local(first.at[pl.ds(512, 128)], w1.at[pl.ds(512, 128)], 8),
        local(first.at[pl.ds(far_at, 512)], w1.at[pl.ds(640, 512)], 9),
    ]
    w2_loads = [
        local(second.at[:, pl.ds(own_at, 512)], w2.at[:, pl.ds(0, 512)], 10),
        local(second.at[:, pl.ds(512, 128)], w2.at[:, pl.ds(512, 128)], 11),
        local(second.at[:, pl.ds(far_at, 512)], w2.at[:, pl.ds(640, 512)], 12),
    ]
    crows_load = local(crows_in, crows, 13)
    srows_load = local(srows_in, srows, 14)
    for copy in (spec_load, ocean_load, wind_load, mask_load, table_load, crows_load):
        copy.start()

    for ref in (es_in, ed_in, e2d_in, sz_in, sx_in, ox_in, oz_in):
        ref[...] = jnp.zeros_like(ref)

    has_s, has_n = gy > 0, gy < ny - 1
    has_w, has_e = gx > 0, gx < nx - 1
    south = {"gy": lax.rem(gy + ny - 1, ny)}
    north = {"gy": lax.rem(gy + 1, ny)}
    west = {"gx": lax.rem(gx + nx - 1, nx)}
    east = {"gx": lax.rem(gx + 1, nx)}
    pair = {"comp": other}
    far_gx = gx + 2 * me - 1
    has_far = jnp.logical_and(far_gx >= 0, far_gx < nx)
    diag = {"comp": other, "gx": lax.rem(far_gx + nx, nx)}
    same_gx = gx + 1 - 2 * me
    has_same = jnp.logical_and(same_gx >= 0, same_gx < nx)
    same = {"gx": lax.rem(same_gx + nx, nx)}

    barrier = pltpu.get_barrier_semaphore()
    greet = ((has_s, south), (has_n, north), (has_w, west), (has_e, east), (has_far, diag))
    other_n, other_s = {**pair, **north}, {**pair, **south}
    greet += ((has_n, other_n), (has_s, other_s))
    for there, place in greet:
        @pl.when(there)
        def _(place=place):
            pl.semaphore_signal(barrier, inc=1, device_id=place, device_id_type=mesh_ids)
    pl.semaphore_signal(barrier, inc=1, device_id=pair, device_id_type=mesh_ids)

    def remote(source, target, send, recv, where):
        return pltpu.make_async_remote_copy(
            src_ref=source, dst_ref=target, send_sem=send, recv_sem=recv,
            device_id=where, device_id_type=mesh_ids,
        )

    ocean_n = remote(oz_out.at[0], oz_in.at[0], oz_send.at[0], oz_recv.at[0], north)
    ocean_s = remote(oz_out.at[1], oz_in.at[1], oz_send.at[1], oz_recv.at[1], south)
    ocean_e = remote(
        ox_out.at[pl.ds(120, 8)], ox_in.at[0, pl.ds(120, 8)], ox_send.at[0], ox_recv.at[0], east
    )
    ocean_w = remote(
        ox_out.at[pl.ds(0, 8)], ox_in.at[1, pl.ds(0, 8)], ox_send.at[1], ox_recv.at[1], west
    )
    swap = [
        [
            remote(
                y_out.at[p, part_of], y_in.at[p, part_of], y_send.at[p, n], y_recv.at[p, n], pair
            )
            for n, part_of in enumerate(SWAP_SLOTS[p])
        ]
        for p in range(2)
    ]
    z1_n = remote(z1_out.at[0], z1_in.at[0], z1_send.at[0], z1_recv.at[0], north)
    z1_s = remote(z1_out.at[1], z1_in.at[1], z1_send.at[1], z1_recv.at[1], south)
    zf_n = [
        remote(y_in.at[0, a], zf_in.at[0, b], zf_send.at[0, n], zf_recv.at[0, n], north)
        for n, (a, b) in enumerate(NORTH_SLOTS)
    ]
    zf_s = [
        remote(y_in.at[0, a], zf_in.at[1, b], zf_send.at[1, n], zf_recv.at[1, n], south)
        for n, (a, b) in enumerate(SOUTH_SLOTS)
    ]
    e_same = remote(es_out, es_in, e1_send.at[0], e1_recv.at[0], same)
    e_diag = remote(ed_out, ed_in, e1_send.at[1], e1_recv.at[1], diag)
    e_pair = remote(ep_out, ep_in, e1_send.at[2], e1_recv.at[2], pair)

    z2 = []
    e2 = []
    for g, tiles in enumerate(GROUPS):
        part_of = pl.ds(PLACED.index(tiles[0]), len(tiles))
        z2.append([
            remote(
                z2_out.at[d, part_of], z2_in.at[d, part_of],
                z2_send.at[d, g], z2_recv.at[d, g], (north, south)[d],
            )
            for d in range(2)
        ])
        e2.append([
            remote(e2d_out.at[g], e2d_in.at[g], e2_send.at[0, g], e2_recv.at[0, g], diag),
            remote(e2p_out.at[g], e2p_in.at[g], e2_send.at[1, g], e2_recv.at[1, g], pair),
        ])
    stress_pair = remote(st_out, st_in, s_send.at[0], s_recv.at[0], pair)
    stress_n = remote(st_out, sz_in.at[0], s_send.at[1], s_recv.at[1], north)
    stress_s = remote(st_out, sz_in.at[1], s_send.at[2], s_recv.at[2], south)
    stress_on = remote(st_out, sx_in.at[0], s_send.at[3], s_recv.at[3], other_n)
    stress_os = remote(st_out, sx_in.at[1], s_send.at[4], s_recv.at[4], other_s)
    final = []
    for h in range(2):
        final.append([])
        for n, (begin, end) in enumerate(FINAL[h]):
            slots = pl.ds(begin, end - begin)
            final[h].append(
                remote(
                    f_out.at[h, slots], f_in.at[h, slots], f_send.at[h, n], f_recv.at[h, n], pair
                )
            )

    def when(condition, *actions):
        @pl.when(condition)
        def _():
            for action in actions:
                action()

    for edge in (0, ROWS + 1):
        state[:, edge, PAD : PAD + HALF] = jnp.zeros((TILES, HALF, TILE), f32)
    spec[:HALF] = jnp.zeros((HALF, ROWS, COLS), f32)
    spec[HALF + comps :] = jnp.zeros((HALF, ROWS, COLS), f32)

    half_is0 = jnp.broadcast_to(me, (HALF, TILE)) == 0
    row_is0 = jnp.broadcast_to(me, (1, TILE)) == 0
    lane = lax.broadcasted_iota(jnp.int32, (HALF, TILE), 1)
    mine = jnp.where(lane < 64, 0, 1) == me

    def pack(first_row, second_row, low_lanes):
        left = jnp.where(low_lanes, first_row, pltpu.roll(first_row, 64, 1))
        right = jnp.where(low_lanes, pltpu.roll(second_row, 64, 1), second_row)
        return jnp.where(lane < 64, left, right).astype(b16)

    def unpack(packed, side, low_lanes):
        wide = packed.astype(f32)
        turned = pltpu.roll(wide, 64, 1)
        if side == 0:
            return jnp.where(low_lanes, wide, turned)
        return jnp.where(low_lanes, turned, wide)

    is_low, is_high = half_is0, jnp.logical_not(half_is0)
    starts = [HALF + me * HALF + TILE * t for t in range(OWN)] + [other * (comps + HALF - 64)]
    spec_load.wait()
    for copy in [cb_load] + w1_loads + w2_loads + [sb_load, srows_load]:
        copy.start()
    counted = [jnp.where(there, 1, 0) for there, _ in greet]

    def y_slot(p, side, t):
        if p == 0:
            return (7, 8, 5, 6)[t] if side else t
        return 1 + 2 * t + side

    def turn(p, side, t):
        r = SWAPPED[p][side]
        turned = spec[pl.ds(starts[t], TILE), r, :].T
        low, high = turned[:HALF], turned[HALF:]
        own = jnp.where(half_is0, low, high)
        far = jnp.where(half_is0, high, low)
        state[t, r + 1, PAD : PAD + HALF] = own
        if t < OWN:
            y_out[p, y_slot(p, side, t)] = far.astype(b16)
        if r == 3:
            z1_out[0, t] = own.astype(b16)
        if r == 0:
            z1_out[1, t] = own.astype(b16)
        at = 4 * t + r
        es_out[at : at + 1] = jnp.where(row_is0, turned[127:128], turned[0:1])
        ed_out[at : at + 1] = jnp.where(row_is0, turned[0:1], turned[127:128])
        ep_out[at : at + 1] = jnp.where(row_is0, turned[63:64], turned[64:65])
        el[at : at + 1] = jnp.where(row_is0, turned[64:65], turned[63:64])
        return far

    for side in range(2):
        for t in (0, 1):
            turn(0, side, t)
        if side == 0:
            pl.semaphore_wait(barrier, 1 + sum(counted))
        swap[0][side].start()
    for side in range(2):
        for t in (2, 3):
            turn(0, side, t)
    y_out[0, 4] = pack(turn(0, 0, 4), turn(0, 1, 4), is_low)
    swap[0][2].start()
    swap[0][3].start()
    when(has_n, z1_n.start)
    when(has_s, z1_s.start)
    for t in range(OWN):
        for side in range(2):
            turn(1, side, t)
    y_out[1, 0] = pack(turn(1, 0, 4), turn(1, 1, 4), is_low)
    swap[1][0].start()
    when(has_far, e_diag.start)
    e_pair.start()
    swap[1][1].start()
    when(has_same, e_same.start)

    ocean_load.wait()
    oz_out[0] = oc[:, ROWS - 1, :]
    oz_out[1] = oc[:, 0, :]
    when(has_n, ocean_n.start)
    when(has_s, ocean_s.start)
    for r in range(ROWS):
        ocat[64 * r : 64 * (r + 1), :] = oc[:, r, :]
    ox_out[...] = ocat[...].T
    when(has_e, ocean_e.start)
    when(has_w, ocean_w.start)

    wind_load.wait()
    mask_load.wait()
    table_load.wait()
    small[...] = jnp.zeros_like(small)
    small[0:4] = msk[...].astype(f32)
    small[4:8] = WIND_GAIN * wnd[0]
    small[8:12] = WIND_GAIN * wnd[1]
    small_t[...] = small[...].T
    columns = small_t[pl.ds(half_at, HALF), :]
    for q in range(3):
        for r in range(ROWS):
            n = 4 * q + r
            at = HALF * ORDER.index(r)
            cells[2 + q, at : at + HALF, :] = jnp.broadcast_to(
                columns[:, n : n + 1], (HALF, TILE)
            )
    cb_load.wait()
    crows_load.wait()
    when(has_s, ocean_n.wait_recv)
    when(has_n, ocean_s.wait_recv)

    def choose(rows_ref, r, b, below, here, above):
        offset = jnp.broadcast_to(rows_ref[b, 0, r] - gy * ROWS - r, (1, COLS))
        return jnp.where(offset < 0, below, jnp.where(offset == 0, here, above))

    for k in range(2):
        at = 16 * k
        lines = [oz_in[0, at : at + 1]]
        lines += [oc[at : at + 1, r, :] for r in range(ROWS)]
        lines += [oz_in[1, at : at + 1]]
        for r in range(ROWS):
            total = cb[r, 0] * choose(crows, r, 0, *lines[r : r + 3])
            total = total + cb[r, 1] * choose(crows, r, 1, *lines[r : r + 3])
            place = HALF * ORDER.index(r)
            cells[k, place : place + HALF, :] = jnp.broadcast_to(
                CURRENT_GAIN * total.sum(axis=1, keepdims=True), (HALF, TILE)
            )

    def edges(t, pair_side, far_side):
        for r in range(ROWS):
            near, far = pair_side[r : r + 1], far_side[r : r + 1]
            state[t, r + 1, PAD - 1 : PAD] = jnp.where(row_is0, far, near)
            state[t, r + 1, PAD + HALF : PAD + HALF + 1] = jnp.where(row_is0, near, far)

    def propagate(tiles, h, fresh, fresh_push):
        def body(i, carry):
            at = pl.multiple_of((2 * h + i) * HALF, HALF)
            r = 3 * i if h else 1 + i
            for lo in (0, 32):
                cell = pl.ds(at + lo, 32)
                cur_x, cur_y, wet, wind_x, wind_y = (cells[q, cell, :] for q in range(5))
                zero = jnp.zeros((32, TILE), f32)
                totals = [
                    zero if (fresh if q < 2 else fresh_push) else sums[q, cell, :]
                    for q in range(4)
                ]
                for t in tiles:
                    speed_x, speed_y, cos, sin, phase, ratio = (
                        tab[t, q : q + 1, :] for q in range(6)
                    )
                    top = PAD + lo
                    here = state[t, r + 1, top : top + 32]
                    before = state[t, r + 1, top - 1 : top + 31]
                    after = state[t, r + 1, top + 1 : top + 33]
                    below = state[t, r, top : top + 32]
                    above = state[t, r + 2, top : top + 32]
                    cx = speed_x + cur_x
                    cy = speed_y + cur_y
                    flux = jnp.abs(cx) * (here - jnp.where(cx > 0.0, before, after))
                    flux = flux + jnp.abs(cy) * (here - jnp.where(cy > 0.0, below, above))
                    moved = wet * (here - flux)
                    growth = jnp.maximum(wind_x * cos + wind_y * sin - phase, 0.0)
                    pushed = growth * moved
                    prop[t, cell, :] = moved
                    rate[t, cell, :] = growth
                    p16[cell, TILE * t : TILE * (t + 1)] = moved.astype(b16)
                    parts = (moved, ratio * moved, pushed * cos, pushed * sin)
                    totals = [a + b for a, b in zip(totals, parts)]
                for q in range(4):
                    sums[q, cell, :] = totals[q]
            return carry

        lax.fori_loop(0, 2, body, 0, unroll=True)

    def finish_sums(rows):
        total = STEPS * comps
        count = rows.stop - rows.start

        def spread(n):
            return jnp.broadcast_to(
                sums[n, rows, :].sum(axis=1, keepdims=True), (count, TILE)
            )

        floor = jnp.maximum(spread(0), 1.0)
        share = spread(1) / floor
        squared[rows] = DECAY_GAIN * share * share
        gain[rows] = (0.5 * total) / floor
        back[rows] = (NONLINEAR_GAIN / total) * floor

    def dot(left, right):
        return lax.dot_general(
            left, right, (((1,), (0,)), ((), ())), preferred_element_type=f32
        )

    def activate(n, pre, rows):
        for j in range(2):
            half = pre[:, TILE * j : TILE * (j + 1)] * gain[rows]
            at = 256 * n + TILE * j
            hidden[rows, at : at + TILE] = (half + half * jnp.tanh(half)).astype(b16)

    def update(tiles, rows):
        at = TILE * tiles[0]
        moved = dot(hidden[rows], w2[:, at : at + TILE * len(tiles)])
        for j, t in enumerate(tiles):
            transfer = moved[:, TILE * j : TILE * (j + 1)].astype(b16).astype(f32)
            fresh = prop[t, rows] * jnp.exp(rate[t, rows] - tab[t, 5:6, :] * squared[rows])
            yield j, t, fresh + back[rows] * transfer

    whole = slice(0, CELLS)
    halves = (slice(0, CELLS // 2), slice(CELLS // 2, CELLS))

    swap[0][0].wait_recv()
    when(has_n, zf_n[0].start)
    swap[0][1].wait_recv()
    when(has_s, zf_s[0].start)
    when(has_s, z1_n.wait_recv)
    when(has_n, z1_s.wait_recv)
    when(has_far, e_same.wait_recv)
    for t in range(OWN):
        edges(t, el[4 * t : 4 * t + 4], es_in[4 * t : 4 * t + 4])
    for d, there in ((0, has_s), (1, has_n)):
        @pl.when(there)
        def _(d=d):
            for t in range(OWN):
                state[t, 5 * d, PAD : PAD + HALF] = z1_in[d, t].astype(f32)
    for h in range(2):
        propagate(range(OWN), h, True, True)
    swap[0][2].wait_recv()
    when(has_n, zf_n[1].start)
    swap[0][3].wait_recv()
    when(has_s, zf_s[1].start)
    for copy in w1_loads:
        copy.wait()
    for n in range(4):
        lanes = slice(256 * n, 256 * (n + 1))
        part[:, lanes] = dot(p16[:, : TILE * OWN], w1[: TILE * OWN, lanes])

    when(has_w, ocean_e.wait_recv)
    when(has_e, ocean_w.wait_recv)
    from_w, from_e = ox_in[0].T, ox_in[1].T
    lane64 = lax.broadcasted_iota(jnp.int32, (64, COLS), 1)
    level64 = lax.rem(lax.broadcasted_iota(jnp.int32, (64, COLS), 0), 16)
    level = lax.broadcasted_iota(jnp.int32, (16, COLS), 0)

    def density(field):
        return HALINE * field[48:64] - THERMAL * field[32:48]

    def pressure(dense):
        running = dense
        for shift in (1, 2, 4, 8):
            running = running + jnp.where(level >= shift, pltpu.roll(running, shift, 0), 0.0)
        return running - 0.5 * dense

    for r in range(ROWS):
        here = oc[:, r, :]
        low = oz_in[0] if r == 0 else oc[:, r - 1, :]
        high = oz_in[1] if r == ROWS - 1 else oc[:, r + 1, :]
        lines = slice(64 * r, 64 * (r + 1))
        left = pltpu.roll(jnp.where(lane64 == COLS - 1, from_w[lines], here), 1, 1)
        right = pltpu.roll(jnp.where(lane64 == 0, from_e[lines], here), COLS - 1, 1)
        upper = jnp.where(level64 == 0, here, pltpu.roll(here, 1, 0))
        lower = jnp.where(level64 == 15, here, pltpu.roll(here, 63, 0))
        mixed = LATERAL_MIX * (left + right + low + high - 4.0 * here)
        mixed = mixed + VERTICAL_MIX * (upper + lower - 2.0 * here)
        across, along = right - left, high - low
        speed_u, speed_v = here[0:16], here[16:32]
        half_gain = 0.5 * PRESSURE_GAIN
        du = CORIOLIS * speed_v - half_gain * pressure(density(across))
        dv = -CORIOLIS * speed_u - half_gain * pressure(density(along))
        pull = -0.5 * ADVECTION
        dtemp = pull * (speed_u * across[32:48] + speed_v * along[32:48])
        dsalt = pull * (speed_u * across[48:64] + speed_v * along[48:64])
        tendency = mixed + jnp.concatenate([du, dv, dtemp, dsalt], axis=0)
        o_out[:, r, :] = here + msk[r : r + 1, :].astype(f32) * tendency


    def merge(p, side, r):
        packed = y_in[p, 4 if p == 0 else 0]
        state[4, r + 1, PAD : PAD + HALF] = jnp.where(
            mine, state[4, r + 1, PAD : PAD + HALF], unpack(packed, side, is_high)
        )

    def arrived(p, side, r, t):
        state[5 + t, r + 1, PAD : PAD + HALF] = y_in[p, y_slot(p, side, t)].astype(f32)

    for side, r in enumerate(SWAPPED[0]):
        for t in range(OWN):
            arrived(0, side, r, t)
        merge(0, side, r)
    for d, there, copy in ((0, has_s, zf_n), (1, has_n, zf_s)):
        @pl.when(there)
        def _(d=d, copy=copy):
            for one in copy:
                one.wait_recv()
            for t in range(OWN):
                at = (3, 4, 1, 2)[t] if d else t
                state[5 + t, 5 * d, PAD : PAD + HALF] = zf_in[d, at].astype(f32)
            state[4, 5 * d, PAD : PAD + HALF] = jnp.where(
                mine, z1_in[d, 4].astype(f32), unpack(zf_in[d, 4 - 4 * d], d, is_high)
            )
    swap[1][0].wait_recv()
    when(has_far, e_diag.wait_recv)
    e_pair.wait_recv()
    for t in range(OWN):
        lines = slice(4 * t, 4 * t + 4)
        edges(5 + t, ep_in[lines], ed_in[lines])
    edges(
        4,
        jnp.where(mine[:4], el[16:20], ep_in[16:20]),
        jnp.where(mine[:4], es_in[16:20], ed_in[16:20]),
    )
    for side, r in enumerate(SWAPPED[1]):
        for t in (0, 1):
            arrived(1, side, r, t)
        merge(1, side, r)
    for h in range(2):
        propagate((4, 5, 6), h, False, False)
    early = slice(TILE * 4, TILE * 7)
    late = slice(TILE * 7, TILE * 9)
    for n in range(4):
        lanes = slice(256 * n, 256 * (n + 1))
        part[:, lanes] = part[:, lanes] + dot(p16[:, early], w1[early, lanes])
    swap[1][1].wait_recv()
    for side, r in enumerate(SWAPPED[1]):
        for t in (2, 3):
            arrived(1, side, r, t)
    for h in range(2):
        propagate((7, 8), h, False, False)
    finish_sums(whole)
    for n in range(4):
        lanes = slice(256 * n, 256 * (n + 1))
        activate(n, part[:, lanes] + dot(p16[:, late], w1[late, lanes]), whole)
    for copy in w2_loads:
        copy.wait()
    for g, products in enumerate(PRODUCTS):
        for tiles in products:
            for _, t, fresh in update(tiles, whole):
                for n, r in enumerate(ORDER):
                    block = fresh[HALF * n : HALF * (n + 1)]
                    state[t, r + 1, PAD : PAD + HALF] = block
                    begin, end = block[:1], block[HALF - 1 :]
                    at = 4 * GROUPS[g].index(t) + r
                    e2d_out[g, at : at + 1] = jnp.where(row_is0, begin, end)
                    e2p_out[g, at : at + 1] = jnp.where(row_is0, end, begin)
                    if r == ROWS - 1:
                        z2_out[0, PLACED.index(t)] = block.astype(b16)
                    if r == 0:
                        z2_out[1, PLACED.index(t)] = block.astype(b16)
        e2[g][1].start()
        when(has_far, e2[g][0].start)
        when(has_n, z2[g][0].start)
        when(has_s, z2[g][1].start)

    def last_update(h, tiles):
        rows = halves[h]
        for _, t, fresh in update(tiles, rows):
            upper, under = fresh[:HALF], fresh[HALF:]
            if t > OWN:
                at = 2 * (t - 5)
                f_out[h, at] = upper.astype(b16)
                f_out[h, at + 1] = under.astype(b16)
            if t == OWN:
                f_out[h, 8] = pack(upper, under, is_high)
            if t <= OWN:
                done[t, rows] = fresh

    def last_sends(h):
        last_update(h, (5, 6))
        final[h][0].start()
        last_update(h, (7, 8))
        if h == 1:
            final[h][1].start()
        last_update(h, (4,))
        final[h][-1].start()

    for g, tiles in enumerate(GROUPS):
        e2[g][1].wait_recv()
        when(has_far, e2[g][0].wait_recv)
        for t in tiles:
            at = 4 * tiles.index(mirror(t))
            edges(t, e2p_in[g, at : at + 4], e2d_in[g, at : at + 4])
        propagate(tiles, 0, g == 0, False)
    finish_sums(halves[0])
    for n in range(4):
        lanes = slice(256 * n, 256 * (n + 1))
        activate(n, dot(p16[halves[0]], w1[:, lanes]), halves[0])
    last_sends(0)

    for g, tiles in enumerate(GROUPS):
        for d, there in ((0, has_s), (1, has_n)):
            @pl.when(there)
            def _(d=d, g=g, tiles=tiles):
                z2[g][d].wait_recv()
                for t in tiles:
                    state[t, 5 * d, PAD : PAD + HALF] = z2_in[d, PLACED.index(t)].astype(f32)
        propagate(tiles, 1, g == 0, False)
    finish_sums(halves[1])
    scale = 1.0 / (STEPS * STEPS * comps)
    packed = jnp.zeros((HALF, TILE), f32)
    for k in range(2):
        for n, r in enumerate(ORDER):
            push = sums[2 + k, HALF * n : HALF * (n + 1), :].sum(axis=1, keepdims=True)
            packed = jnp.where(lane == 4 * k + r, scale * push, packed)
    small[...] = jnp.zeros_like(small)
    small[pl.ds(half_at, HALF), :] = packed
    small_t[...] = small[...].T
    st_out[...] = small_t[0:8]
    stress_pair.start()
    when(has_n, stress_n.start, stress_on.start)
    when(has_s, stress_s.start, stress_os.start)
    for n in range(4):
        lanes = slice(256 * n, 256 * (n + 1))
        activate(n, dot(p16[halves[1]], w1[:, lanes]), halves[1])
    last_sends(1)
    for h in range(2):
        for tiles in ((0, 1), (2, 3)):
            last_update(h, tiles)
    stress_pair.wait_recv()
    st_full[...] = st_out[...] + st_in[...]

    def turn_back(h, t):
        for side in range(2):
            n = 2 * h + side
            own = done[t, HALF * n : HALF * (n + 1)]
            if t < OWN:
                came = f_in[h, 2 * t + side].astype(f32)
            else:
                came = unpack(f_in[h, 8], side, is_low)
            turned = jnp.concatenate(
                [jnp.where(half_is0, own, came), jnp.where(half_is0, came, own)], axis=0
            ).T
            r = ORDER[n]
            if t < OWN:
                out[pl.ds(me * HALF + TILE * t, TILE), r, :] = turned
            else:
                out[pl.ds(other * (comps - HALF), HALF), r, :] = jnp.where(
                    half_is0, turned[:HALF], turned[HALF:]
                )

    final[0][0].wait_recv()
    for t in (0, 1):
        turn_back(0, t)
    final[0][1].wait_recv()
    for t in (2, 3, 4):
        turn_back(0, t)

    sb_load.wait()
    srows_load.wait()
    when(has_s, stress_n.wait_recv, stress_on.wait_recv)
    when(has_n, stress_s.wait_recv, stress_os.wait_recv)
    beyond = [sz_in[d] + sx_in[d] for d in range(2)]
    for k in range(2):
        lines = [beyond[0][4 * k + 3 : 4 * k + 4]]
        lines += [st_full[4 * k + r : 4 * k + r + 1] for r in range(ROWS)]
        lines += [beyond[1][4 * k : 4 * k + 1]]
        for r in range(ROWS):
            total = sb[r, 0] * choose(srows, r, 0, *lines[r : r + 3])
            total = total + sb[r, 1] * choose(srows, r, 1, *lines[r : r + 3])
            stress = total.T.sum(axis=0, keepdims=True)
            wet = msk[r : r + 1, :].astype(f32)
            at = 16 * k
            o_out[at : at + 1, r, :] = o_out[at : at + 1, r, :] + wet * (STRESS_GAIN * stress)

    for n, tiles in enumerate(((0, 1), (2, 3), (4,))):
        final[1][n].wait_recv()
        for t in tiles:
            turn_back(1, t)

    when(has_n, ocean_n.wait_send, z1_n.wait_send, stress_n.wait_send, stress_on.wait_send)
    when(has_s, ocean_s.wait_send, z1_s.wait_send, stress_s.wait_send, stress_os.wait_send)
    for n in range(2):
        when(has_n, zf_n[n].wait_send)
        when(has_s, zf_s[n].wait_send)
    when(has_e, ocean_e.wait_send)
    when(has_w, ocean_w.wait_send)
    when(has_same, e_same.wait_send)
    when(has_far, e_diag.wait_send)
    for copy in swap[0] + swap[1] + [e_pair, stress_pair] + final[0] + final[1]:
        copy.wait_send()
    for g in range(len(GROUPS)):
        when(has_n, z2[g][0].wait_send)
        when(has_s, z2[g][1].wait_send)
        when(has_far, e2[g][0].wait_send)
        e2[g][1].wait_send()


def kernel_call(
    spectra, first, second, table, ocean, wind, mask, cblocks, sblocks, crows, srows
):
    f32, b16 = jnp.float32, jnp.bfloat16
    comps = spectra.shape[0]
    units = first.shape[1]
    total = TILE * TILES
    shape = jax.ShapeDtypeStruct
    dma = pltpu.SemaphoreType.DMA
    groups = len(GROUPS)
    vmem = pltpu.VMEM
    scratch = [
        vmem((comps + 2 * HALF, ROWS, COLS), f32),
        vmem((total, units), b16),
        vmem((units, total), b16),
        vmem((TILES, 8, TILE), f32),
        vmem(ocean.shape, f32),
        vmem(wind.shape, f32),
        vmem(mask.shape, jnp.int32),
        vmem((ROWS, 2, HALF, COLS), f32),
        vmem((ROWS, 2, COLS, COLS), f32),
        vmem((TILES, ROWS + 2, HALF + 2 * PAD, TILE), f32),
        vmem((TILES, CELLS, TILE), f32),
        vmem((TILES, CELLS, TILE), f32),
        vmem((CELLS, total), b16),
        vmem((CELLS, units), f32),
        vmem((CELLS, units), b16),
        vmem((4, CELLS, TILE), f32),
        vmem((5, CELLS, TILE), f32),
        vmem((CELLS, TILE), f32),
        vmem((CELLS, TILE), f32),
        vmem((CELLS, TILE), f32),
        vmem((TILE, TILE), f32),
        vmem((TILE, TILE), f32),
        vmem((2, TILES, HALF, TILE), b16),
        vmem((2, TILES, HALF, TILE), b16),
        vmem((2, OWN + 1, HALF, TILE), b16),
        vmem((2, OWN + 1, HALF, TILE), b16),
        vmem((2, OWN + 1, HALF, TILE), b16),
        *[vmem((24, TILE), f32) for _ in range(7)],
        vmem((2, TILES, HALF, TILE), b16),
        vmem((2, TILES, HALF, TILE), b16),
        *[vmem((groups, 24, TILE), f32) for _ in range(4)],
        vmem((2, 64, COLS), f32),
        vmem((2, 64, COLS), f32),
        vmem((256, COLS), f32),
        vmem((COLS, 256), f32),
        vmem((2, COLS, 256), f32),
        vmem((8, COLS), f32),
        vmem((8, COLS), f32),
        vmem((8, COLS), f32),
        vmem((2, 8, COLS), f32),
        vmem((2, 8, COLS), f32),
        vmem((2, TILES, HALF, TILE), b16),
        vmem((2, TILES, HALF, TILE), b16),
        vmem((OWN + 1, CELLS, TILE), f32),
        pltpu.SMEM((2, 1, ROWS), jnp.int32),
        pltpu.SMEM((2, 1, ROWS), jnp.int32),
        dma((15,)),
        dma((2,)), dma((2,)),
        dma((2,)), dma((2,)),
        dma((2, 4)), dma((2, 4)),
        dma((2,)), dma((2,)),
        dma((2, 2)), dma((2, 2)),
        dma((3,)), dma((3,)),
        dma((2, groups)), dma((2, groups)),
        dma((2, groups)), dma((2, groups)),
        dma((5,)), dma((5,)),
        dma((2, 3)), dma((2, 3)),
    ]
    return pl.pallas_call(
        kernel,
        out_shape=(shape(spectra.shape, f32), shape(ocean.shape, f32)),
        in_specs=[pl.BlockSpec(memory_space=pl.ANY)] * 11,
        out_specs=(pl.BlockSpec(memory_space=pltpu.VMEM),) * 2,
        scratch_shapes=scratch,
        compiler_params=pltpu.CompilerParams(
            vmem_limit_bytes=VMEM_LIMIT, collective_id=0, has_side_effects=True
        ),
    )(*(
        pltpu.with_memory_space_constraint(x, pltpu.HBM)
        for x in (
            spectra, first, second, table, ocean, wind, mask, cblocks, sblocks, crows, srows
        )
    ))


PIECES = 4


def place_kernel(a, b, a_out, b_out, sems):
    rows = a.shape[0] // PIECES
    copies = [pltpu.make_async_copy(b, b_out, sems.at[PIECES])]
    for n in range(PIECES):
        part = pl.ds(n * rows, rows)
        copies.append(pltpu.make_async_copy(a.at[part], a_out.at[part], sems.at[n]))
    for copy in copies:
        copy.start()
    for copy in copies:
        copy.wait()


def place_call(a, b):
    shape = jax.ShapeDtypeStruct
    return pl.pallas_call(
        place_kernel,
        out_shape=(shape(a.shape, a.dtype), shape(b.shape, b.dtype)),
        in_specs=[pl.BlockSpec(memory_space=pl.ANY)] * 2,
        out_specs=(pl.BlockSpec(memory_space=pl.ANY),) * 2,
        scratch_shapes=[pltpu.SemaphoreType.DMA((PIECES + 1,))],
        compiler_params=pltpu.CompilerParams(vmem_limit_bytes=VMEM_LIMIT),
    )(a, b)


def local_step(
    spectra,
    wind_field,
    sea_mask,
    first_layer,
    second_layer,
    ocean_state,
    current_blocks,
    current_rows,
    stress_blocks,
    stress_rows,
):
    half_freqs, directions, rows, cols = spectra.shape
    variables, levels = ocean_state.shape[:2]
    table = jnp.asarray(tables(2 * half_freqs, directions))
    state, ocean = kernel_call(
        spectra.reshape(half_freqs * directions, rows, cols),
        first_layer,
        second_layer,
        table,
        ocean_state.reshape(variables * levels, rows, cols),
        wind_field,
        sea_mask,
        current_blocks,
        stress_blocks,
        current_rows.transpose(1, 2, 0),
        stress_rows.transpose(1, 2, 0),
    )
    state, ocean = place_call(state, ocean)
    return state.reshape(spectra.shape), ocean.reshape(ocean_state.shape)


def solution(mesh):
    placed = (
        P("comp", None, "gy", "gx"),
        P(None, "gy", "gx"),
        P("gy", "gx"),
        P(),
        P(),
        P(None, None, "gy", "gx"),
        P("gy", None, "gx", None),
        P("gy", None, "gx"),
        P("gy", None, "gx", None),
        P("gy", None, "gx"),
    )
    return jax.shard_map(
        local_step,
        mesh=mesh,
        in_specs=placed,
        out_specs=(P("comp", None, "gy", "gx"), P(None, None, "gy", "gx")),
        check_vma=False,
    )
```

```python
import numpy as np

import jax
import jax.numpy as jnp
from jax import lax
from jax.experimental import pallas as pl
from jax.experimental.pallas import tpu as pltpu
from jax.sharding import PartitionSpec as P

CURRENT_GAIN = 0.08
WIND_GAIN = 0.06
DECAY_GAIN = 0.03
NONLINEAR_GAIN = 0.3
THERMAL = 0.2
HALINE = 0.8
CORIOLIS = 0.1
PRESSURE_GAIN = 0.2
LATERAL_MIX = 0.1
VERTICAL_MIX = 0.2
ADVECTION = 0.3
STRESS_GAIN = 150.0

STEPS = 2
ROWS = 4
COLS = 128
HALF = 64
CELLS = ROWS * HALF
TILE = 128
TILES = 9
OWN = 4
PAD = 8
GROUPS = ((0, 1, 5, 6), (2, 3, 7, 8, 4))
PLACED = GROUPS[0] + GROUPS[1]
PRODUCTS = (((0, 1), (5, 6)), ((2, 3), (7, 8), (4,)))
SWAP_SLOTS = (
    (pl.ds(0, 2), pl.ds(7, 2), pl.ds(2, 3), pl.ds(5, 2)),
    (pl.ds(0, 5), pl.ds(5, 4)),
)
NORTH_SLOTS = ((pl.ds(0, 2), pl.ds(0, 2)), (pl.ds(2, 3), pl.ds(2, 3)))
SOUTH_SLOTS = ((pl.ds(7, 2), pl.ds(3, 2)), (pl.ds(4, 3), pl.ds(0, 3)))
ORDER = (1, 2, 0, 3)
SWAPPED = ((3, 0), (1, 2))
FINAL = (((0, 4), (4, 9)), ((0, 4), (4, 8), (8, 9)))
VMEM_LIMIT = 32 * 1024 * 1024


def tables(total, directions):
    index = np.arange(total, dtype=np.float64)
    group = 0.4 * np.exp(-3.0 * index / (total - 1))
    ratio = np.exp(2.0 * index / (total - 1) - 1.0)
    angles = 2.0 * np.pi * np.arange(directions) / directions
    cosines, sines = np.cos(angles), np.sin(angles)
    full = np.zeros((8, total, directions))
    full[0] = group[:, None] * cosines
    full[1] = group[:, None] * sines
    full[2] = cosines
    full[3] = sines
    full[4] = WIND_GAIN * 4.0 * group[:, None]
    full[5] = ratio[:, None]
    tiled = full.reshape(8, TILES, TILE).transpose(1, 0, 2)
    swapped = np.concatenate([tiled[5:], tiled[4:5], tiled[:4]])
    return np.stack([tiled, swapped]).astype(np.float32)


def mirror(t):
    return 4 if t == 4 else (t + 5) % 10


def kernel(
    spectra, first, second, table, ocean, wind, mask, cblocks, sblocks, crows_in, srows_in,
    out, o_out,
    spec, w1, w2, tab, oc, wnd, msk, cb, sb,
    state, later, prop, rate, p16, part, hidden, sums, cells, gain, back, squared, small, small_t,
    y_out, y_in, z1_out, z1_in, zf_in, es_out, es_in, ed_out, ed_in, ep_out, ep_in, el,
    z2_out, z2_in, e2d_out, e2d_in, e2p_out, e2p_in,
    oz_out, oz_in, ocat, ox_out, ox_in, st_out, st_in, st_full, sz_in, sx_in, f_out, f_in, done,
    crows, srows, load, oz_send, oz_recv, ox_send, ox_recv, y_send, y_recv, z1_send, z1_recv,
    zf_send, zf_recv, e1_send, e1_recv, z2_send, z2_recv, e2_send, e2_recv,
    s_send, s_recv, f_send, f_recv,
):
    f32, b16 = jnp.float32, jnp.bfloat16
    me = lax.axis_index("comp")
    other = 1 - me
    gy, ny = lax.axis_index("gy"), lax.axis_size("gy")
    gx, nx = lax.axis_index("gx"), lax.axis_size("gx")
    comps = spectra.shape[0]
    mesh_ids = pl.DeviceIdType.MESH

    def local(source, target, n):
        return pltpu.make_async_copy(source, target, load.at[n])

    own_at = pl.multiple_of(me * 5 * TILE, TILE)
    far_at = pl.multiple_of(other * 5 * TILE, TILE)
    half_at = pl.multiple_of(me * HALF, HALF)
    spec_load = local(spectra, spec.at[pl.ds(HALF, comps)], 0)
    ocean_load = local(ocean, oc, 1)
    wind_load = local(wind, wnd, 2)
    mask_load = local(mask, msk, 3)
    table_load = local(table.at[me], tab, 4)
    cb_load = local(cblocks.at[:, :, pl.ds(half_at, HALF), :], cb, 5)
    sb_load = local(sblocks, sb, 6)
    w1_loads = [
        local(first.at[pl.ds(own_at, 512)], w1.at[pl.ds(0, 512)], 7),
        local(first.at[pl.ds(512, 128)], w1.at[pl.ds(512, 128)], 8),
        local(first.at[pl.ds(far_at, 512)], w1.at[pl.ds(640, 512)], 9),
    ]
    w2_loads = [
        local(second.at[:, pl.ds(own_at, 512)], w2.at[:, pl.ds(0, 512)], 10),
        local(second.at[:, pl.ds(512, 128)], w2.at[:, pl.ds(512, 128)], 11),
        local(second.at[:, pl.ds(far_at, 512)], w2.at[:, pl.ds(640, 512)], 12),
    ]
    crows_load = local(crows_in, crows, 13)
    srows_load = local(srows_in, srows, 14)
    for copy in (spec_load, ocean_load, wind_load, mask_load, table_load, crows_load):
        copy.start()

    for ref in (es_in, ed_in, e2d_in, sz_in, sx_in, ox_in, oz_in):
        ref[...] = jnp.zeros_like(ref)

    has_s, has_n = gy > 0, gy < ny - 1
    has_w, has_e = gx > 0, gx < nx - 1
    south = {"gy": lax.rem(gy + ny - 1, ny)}
    north = {"gy": lax.rem(gy + 1, ny)}
    west = {"gx": lax.rem(gx + nx - 1, nx)}
    east = {"gx": lax.rem(gx + 1, nx)}
    pair = {"comp": other}
    far_gx = gx + 2 * me - 1
    has_far = jnp.logical_and(far_gx >= 0, far_gx < nx)
    diag = {"comp": other, "gx": lax.rem(far_gx + nx, nx)}
    same_gx = gx + 1 - 2 * me
    has_same = jnp.logical_and(same_gx >= 0, same_gx < nx)
    same = {"gx": lax.rem(same_gx + nx, nx)}

    barrier = pltpu.get_barrier_semaphore()
    greet = ((has_s, south), (has_n, north), (has_w, west), (has_e, east), (has_far, diag))
    other_n, other_s = {**pair, **north}, {**pair, **south}
    greet += ((has_n, other_n), (has_s, other_s))
    for there, place in greet:
        @pl.when(there)
        def _(place=place):
            pl.semaphore_signal(barrier, inc=1, device_id=place, device_id_type=mesh_ids)
    pl.semaphore_signal(barrier, inc=1, device_id=pair, device_id_type=mesh_ids)

    def remote(source, target, send, recv, where):
        return pltpu.make_async_remote_copy(
            src_ref=source, dst_ref=target, send_sem=send, recv_sem=recv,
            device_id=where, device_id_type=mesh_ids,
        )

    ocean_n = remote(oz_out.at[0], oz_in.at[0], oz_send.at[0], oz_recv.at[0], north)
    ocean_s = remote(oz_out.at[1], oz_in.at[1], oz_send.at[1], oz_recv.at[1], south)
    ocean_e = remote(
        ox_out.at[pl.ds(120, 8)], ox_in.at[0, pl.ds(120, 8)], ox_send.at[0], ox_recv.at[0], east
    )
    ocean_w = remote(
        ox_out.at[pl.ds(0, 8)], ox_in.at[1, pl.ds(0, 8)], ox_send.at[1], ox_recv.at[1], west
    )
    swap = [
        [
            remote(
                y_out.at[p, part_of], y_in.at[p, part_of], y_send.at[p, n], y_recv.at[p, n], pair
            )
            for n, part_of in enumerate(SWAP_SLOTS[p])
        ]
        for p in range(2)
    ]
    z1_n = remote(z1_out.at[0], z1_in.at[0], z1_send.at[0], z1_recv.at[0], north)
    z1_s = remote(z1_out.at[1], z1_in.at[1], z1_send.at[1], z1_recv.at[1], south)
    zf_n = [
        remote(y_in.at[0, a], zf_in.at[0, b], zf_send.at[0, n], zf_recv.at[0, n], north)
        for n, (a, b) in enumerate(NORTH_SLOTS)
    ]
    zf_s = [
        remote(y_in.at[0, a], zf_in.at[1, b], zf_send.at[1, n], zf_recv.at[1, n], south)
        for n, (a, b) in enumerate(SOUTH_SLOTS)
    ]
    e_same = remote(es_out, es_in, e1_send.at[0], e1_recv.at[0], same)
    e_diag = remote(ed_out, ed_in, e1_send.at[1], e1_recv.at[1], diag)
    e_pair = remote(ep_out, ep_in, e1_send.at[2], e1_recv.at[2], pair)

    z2 = []
    e2 = []
    for g, tiles in enumerate(GROUPS):
        part_of = pl.ds(PLACED.index(tiles[0]), len(tiles))
        z2.append([
            remote(
                z2_out.at[d, part_of], z2_in.at[d, part_of],
                z2_send.at[d, g], z2_recv.at[d, g], (north, south)[d],
            )
            for d in range(2)
        ])

    for h in range(2):
        e2.append([
            remote(e2d_out.at[h], e2d_in.at[h], e2_send.at[0, h], e2_recv.at[0, h], diag),
            remote(e2p_out.at[h], e2p_in.at[h], e2_send.at[1, h], e2_recv.at[1, h], pair),
        ])
    stress_pair = remote(st_out, st_in, s_send.at[0], s_recv.at[0], pair)
    stress_n = remote(st_out, sz_in.at[0], s_send.at[1], s_recv.at[1], north)
    stress_s = remote(st_out, sz_in.at[1], s_send.at[2], s_recv.at[2], south)
    stress_on = remote(st_out, sx_in.at[0], s_send.at[3], s_recv.at[3], other_n)
    stress_os = remote(st_out, sx_in.at[1], s_send.at[4], s_recv.at[4], other_s)
    final = []
    for h in range(2):
        final.append([])
        for n, (begin, end) in enumerate(FINAL[h]):
            slots = pl.ds(begin, end - begin)
            final[h].append(
                remote(
                    f_out.at[h, slots], f_in.at[h, slots], f_send.at[h, n], f_recv.at[h, n], pair
                )
            )

    def when(condition, *actions):
        @pl.when(condition)
        def _():
            for action in actions:
                action()

    for edge in (0, ROWS + 1):
        for field in (state, later):
            field[:, edge, PAD : PAD + HALF] = jnp.zeros((TILES, HALF, TILE), f32)
    spec[:HALF] = jnp.zeros((HALF, ROWS, COLS), f32)
    spec[HALF + comps :] = jnp.zeros((HALF, ROWS, COLS), f32)

    half_is0 = jnp.broadcast_to(me, (HALF, TILE)) == 0
    row_is0 = jnp.broadcast_to(me, (1, TILE)) == 0
    lane = lax.broadcasted_iota(jnp.int32, (HALF, TILE), 1)
    mine = jnp.where(lane < 64, 0, 1) == me

    def pack(first_row, second_row, low_lanes):
        left = jnp.where(low_lanes, first_row, pltpu.roll(first_row, 64, 1))
        right = jnp.where(low_lanes, pltpu.roll(second_row, 64, 1), second_row)
        return jnp.where(lane < 64, left, right).astype(b16)

    def unpack(packed, side, low_lanes):
        wide = packed.astype(f32)
        turned = pltpu.roll(wide, 64, 1)
        if side == 0:
            return jnp.where(low_lanes, wide, turned)
        return jnp.where(low_lanes, turned, wide)

    is_low, is_high = half_is0, jnp.logical_not(half_is0)
    starts = [HALF + me * HALF + TILE * t for t in range(OWN)] + [other * (comps + HALF - 64)]
    spec_load.wait()
    for copy in [cb_load] + w1_loads + w2_loads + [sb_load, srows_load]:
        copy.start()
    counted = [jnp.where(there, 1, 0) for there, _ in greet]

    def y_slot(p, side, t):
        if p == 0:
            return (7, 8, 5, 6)[t] if side else t
        return 1 + 2 * t + side

    def turn(p, side, t):
        r = SWAPPED[p][side]
        turned = spec[pl.ds(starts[t], TILE), r, :].T
        low, high = turned[:HALF], turned[HALF:]
        own = jnp.where(half_is0, low, high)
        far = jnp.where(half_is0, high, low)
        state[t, r + 1, PAD : PAD + HALF] = own
        if t < OWN:
            y_out[p, y_slot(p, side, t)] = far.astype(b16)
        if r == 3:
            z1_out[0, t] = own.astype(b16)
        if r == 0:
            z1_out[1, t] = own.astype(b16)
        at = 4 * t + r
        es_out[at : at + 1] = jnp.where(row_is0, turned[127:128], turned[0:1])
        ed_out[at : at + 1] = jnp.where(row_is0, turned[0:1], turned[127:128])
        ep_out[at : at + 1] = jnp.where(row_is0, turned[63:64], turned[64:65])
        el[at : at + 1] = jnp.where(row_is0, turned[64:65], turned[63:64])
        return far

    for side in range(2):
        for t in (0, 1):
            turn(0, side, t)
        if side == 0:
            pl.semaphore_wait(barrier, 1 + sum(counted))
        swap[0][side].start()
    for side in range(2):
        for t in (2, 3):
            turn(0, side, t)
    y_out[0, 4] = pack(turn(0, 0, 4), turn(0, 1, 4), is_low)
    swap[0][2].start()
    swap[0][3].start()
    when(has_n, z1_n.start)
    when(has_s, z1_s.start)
    for t in range(OWN):
        for side in range(2):
            turn(1, side, t)
    y_out[1, 0] = pack(turn(1, 0, 4), turn(1, 1, 4), is_low)
    swap[1][0].start()
    when(has_far, e_diag.start)
    e_pair.start()
    swap[1][1].start()
    when(has_same, e_same.start)

    ocean_load.wait()
    oz_out[0] = oc[:, ROWS - 1, :]
    oz_out[1] = oc[:, 0, :]
    when(has_n, ocean_n.start)
    when(has_s, ocean_s.start)
    for r in range(ROWS):
        ocat[64 * r : 64 * (r + 1), :] = oc[:, r, :]
    ox_out[...] = ocat[...].T
    when(has_e, ocean_e.start)
    when(has_w, ocean_w.start)

    wind_load.wait()
    mask_load.wait()
    table_load.wait()
    small[...] = jnp.zeros_like(small)
    small[0:4] = msk[...].astype(f32)
    small[4:8] = WIND_GAIN * wnd[0]
    small[8:12] = WIND_GAIN * wnd[1]
    small_t[...] = small[...].T
    columns = small_t[pl.ds(half_at, HALF), :]
    for q in range(3):
        for r in range(ROWS):
            n = 4 * q + r
            at = HALF * ORDER.index(r)
            cells[2 + q, at : at + HALF, :] = jnp.broadcast_to(
                columns[:, n : n + 1], (HALF, TILE)
            )
    cb_load.wait()
    crows_load.wait()
    when(has_s, ocean_n.wait_recv)
    when(has_n, ocean_s.wait_recv)

    def choose(rows_ref, r, b, below, here, above):
        offset = jnp.broadcast_to(rows_ref[b, 0, r] - gy * ROWS - r, (1, COLS))
        return jnp.where(offset < 0, below, jnp.where(offset == 0, here, above))

    for k in range(2):
        at = 16 * k
        lines = [oz_in[0, at : at + 1]]
        lines += [oc[at : at + 1, r, :] for r in range(ROWS)]
        lines += [oz_in[1, at : at + 1]]
        for r in range(ROWS):
            total = cb[r, 0] * choose(crows, r, 0, *lines[r : r + 3])
            total = total + cb[r, 1] * choose(crows, r, 1, *lines[r : r + 3])
            place = HALF * ORDER.index(r)
            cells[k, place : place + HALF, :] = jnp.broadcast_to(
                CURRENT_GAIN * total.sum(axis=1, keepdims=True), (HALF, TILE)
            )

    def edges(field, t, rows, pair_side, far_side):
        for n, r in enumerate(rows):
            near, away = pair_side[n : n + 1], far_side[n : n + 1]
            field[t, r + 1, PAD - 1 : PAD] = jnp.where(row_is0, away, near)
            field[t, r + 1, PAD + HALF : PAD + HALF + 1] = jnp.where(row_is0, near, away)

    def propagate(field, tiles, h, fresh, fresh_push):
        def body(i, carry):
            at = pl.multiple_of((2 * h + i) * HALF, HALF)
            r = 3 * i if h else 1 + i
            for lo in (0, 32):
                cell = pl.ds(at + lo, 32)
                cur_x, cur_y, wet, wind_x, wind_y = (cells[q, cell, :] for q in range(5))
                zero = jnp.zeros((32, TILE), f32)
                totals = [
                    zero if (fresh if q < 2 else fresh_push) else sums[q, cell, :]
                    for q in range(4)
                ]
                for t in tiles:
                    speed_x, speed_y, cos, sin, phase, ratio = (
                        tab[t, q : q + 1, :] for q in range(6)
                    )
                    top = PAD + lo
                    here = field[t, r + 1, top : top + 32]
                    before = field[t, r + 1, top - 1 : top + 31]
                    after = field[t, r + 1, top + 1 : top + 33]
                    below = field[t, r, top : top + 32]
                    above = field[t, r + 2, top : top + 32]
                    cx = speed_x + cur_x
                    cy = speed_y + cur_y
                    flux = jnp.abs(cx) * (here - jnp.where(cx > 0.0, before, after))
                    flux = flux + jnp.abs(cy) * (here - jnp.where(cy > 0.0, below, above))
                    moved = wet * (here - flux)
                    growth = jnp.maximum(wind_x * cos + wind_y * sin - phase, 0.0)
                    pushed = growth * moved
                    prop[t, cell, :] = moved
                    rate[t, cell, :] = growth
                    p16[cell, TILE * t : TILE * (t + 1)] = moved.astype(b16)
                    parts = (moved, ratio * moved, pushed * cos, pushed * sin)
                    totals = [a + b for a, b in zip(totals, parts)]
                for q in range(4):
                    sums[q, cell, :] = totals[q]
            return carry

        lax.fori_loop(0, 2, body, 0, unroll=True)

    def finish_sums(rows):
        total = STEPS * comps
        count = rows.stop - rows.start

        def spread(n):
            return jnp.broadcast_to(
                sums[n, rows, :].sum(axis=1, keepdims=True), (count, TILE)
            )

        floor = jnp.maximum(spread(0), 1.0)
        share = spread(1) / floor
        squared[rows] = DECAY_GAIN * share * share
        gain[rows] = (0.5 * total) / floor
        back[rows] = (NONLINEAR_GAIN / total) * floor

    def dot(left, right):
        return lax.dot_general(
            left, right, (((1,), (0,)), ((), ())), preferred_element_type=f32
        )

    def activate(n, pre, rows):
        for j in range(2):
            half = pre[:, TILE * j : TILE * (j + 1)] * gain[rows]
            at = 256 * n + TILE * j
            hidden[rows, at : at + TILE] = (half + half * jnp.tanh(half)).astype(b16)

    def update(tiles, rows):
        at = TILE * tiles[0]
        moved = dot(hidden[rows], w2[:, at : at + TILE * len(tiles)])
        for j, t in enumerate(tiles):
            transfer = moved[:, TILE * j : TILE * (j + 1)].astype(b16).astype(f32)
            fresh = prop[t, rows] * jnp.exp(rate[t, rows] - tab[t, 5:6, :] * squared[rows])
            yield j, t, fresh + back[rows] * transfer

    whole = slice(0, CELLS)
    halves = (slice(0, CELLS // 2), slice(CELLS // 2, CELLS))

    swap[0][0].wait_recv()
    when(has_n, zf_n[0].start)
    swap[0][1].wait_recv()
    when(has_s, zf_s[0].start)
    when(has_s, z1_n.wait_recv)
    when(has_n, z1_s.wait_recv)
    when(has_far, e_same.wait_recv)
    for t in range(OWN):
        edges(state, t, range(4), el[4 * t : 4 * t + 4], es_in[4 * t : 4 * t + 4])
    for d, there in ((0, has_s), (1, has_n)):
        @pl.when(there)
        def _(d=d):
            for t in range(OWN):
                state[t, 5 * d, PAD : PAD + HALF] = z1_in[d, t].astype(f32)
    for h in range(2):
        propagate(state, range(OWN), h, True, True)
    swap[0][2].wait_recv()
    when(has_n, zf_n[1].start)
    swap[0][3].wait_recv()
    when(has_s, zf_s[1].start)
    for copy in w1_loads:
        copy.wait()
    for n in range(4):
        lanes = slice(256 * n, 256 * (n + 1))
        part[:, lanes] = dot(p16[:, : TILE * OWN], w1[: TILE * OWN, lanes])

    when(has_w, ocean_e.wait_recv)
    when(has_e, ocean_w.wait_recv)
    from_w, from_e = ox_in[0].T, ox_in[1].T
    lane64 = lax.broadcasted_iota(jnp.int32, (64, COLS), 1)
    level64 = lax.rem(lax.broadcasted_iota(jnp.int32, (64, COLS), 0), 16)
    level = lax.broadcasted_iota(jnp.int32, (16, COLS), 0)

    def density(field):
        return HALINE * field[48:64] - THERMAL * field[32:48]

    def pressure(dense):
        running = dense
        for shift in (1, 2, 4, 8):
            running = running + jnp.where(level >= shift, pltpu.roll(running, shift, 0), 0.0)
        return running - 0.5 * dense

    for r in range(ROWS):
        here = oc[:, r, :]
        low = oz_in[0] if r == 0 else oc[:, r - 1, :]
        high = oz_in[1] if r == ROWS - 1 else oc[:, r + 1, :]
        lines = slice(64 * r, 64 * (r + 1))
        left = pltpu.roll(jnp.where(lane64 == COLS - 1, from_w[lines], here), 1, 1)
        right = pltpu.roll(jnp.where(lane64 == 0, from_e[lines], here), COLS - 1, 1)
        upper = jnp.where(level64 == 0, here, pltpu.roll(here, 1, 0))
        lower = jnp.where(level64 == 15, here, pltpu.roll(here, 63, 0))
        mixed = LATERAL_MIX * (left + right + low + high - 4.0 * here)
        mixed = mixed + VERTICAL_MIX * (upper + lower - 2.0 * here)
        across, along = right - left, high - low
        speed_u, speed_v = here[0:16], here[16:32]
        half_gain = 0.5 * PRESSURE_GAIN
        du = CORIOLIS * speed_v - half_gain * pressure(density(across))
        dv = -CORIOLIS * speed_u - half_gain * pressure(density(along))
        pull = -0.5 * ADVECTION
        dtemp = pull * (speed_u * across[32:48] + speed_v * along[32:48])
        dsalt = pull * (speed_u * across[48:64] + speed_v * along[48:64])
        tendency = mixed + jnp.concatenate([du, dv, dtemp, dsalt], axis=0)
        o_out[:, r, :] = here + msk[r : r + 1, :].astype(f32) * tendency


    def merge(p, side, r):
        packed = y_in[p, 4 if p == 0 else 0]
        state[4, r + 1, PAD : PAD + HALF] = jnp.where(
            mine, state[4, r + 1, PAD : PAD + HALF], unpack(packed, side, is_high)
        )

    def arrived(p, side, r, t):
        state[5 + t, r + 1, PAD : PAD + HALF] = y_in[p, y_slot(p, side, t)].astype(f32)

    for side, r in enumerate(SWAPPED[0]):
        for t in range(OWN):
            arrived(0, side, r, t)
        merge(0, side, r)
    swap[1][0].wait_recv()
    when(has_far, e_diag.wait_recv)
    e_pair.wait_recv()
    for t in range(OWN):
        lines = slice(4 * t, 4 * t + 4)
        edges(state, 5 + t, range(4), ep_in[lines], ed_in[lines])
    edges(
        state,
        4,
        range(4),
        jnp.where(mine[:4], el[16:20], ep_in[16:20]),
        jnp.where(mine[:4], es_in[16:20], ed_in[16:20]),
    )
    for side, r in enumerate(SWAPPED[1]):
        for t in (0, 1):
            arrived(1, side, r, t)
        merge(1, side, r)
    propagate(state, (4, 5, 6), 0, False, False)
    early = slice(TILE * 4, TILE * 7)
    late = slice(TILE * 7, TILE * 9)
    for n in range(4):
        lanes = slice(256 * n, 256 * (n + 1))
        extra = dot(p16[halves[0], early], w1[early, lanes])
        part[halves[0], lanes] = part[halves[0], lanes] + extra
    swap[1][1].wait_recv()
    for side, r in enumerate(SWAPPED[1]):
        for t in (2, 3):
            arrived(1, side, r, t)
    propagate(state, (7, 8), 0, False, False)

    def first_network(h, taken):
        rows = halves[h]
        finish_sums(rows)
        for n in range(4):
            lanes = slice(256 * n, 256 * (n + 1))
            activate(n, part[rows, lanes] + dot(p16[rows, taken], w1[taken, lanes]), rows)

    def first_update(h, products):
        for tiles in products:
            for _, t, fresh in update(tiles, halves[h]):
                for side in range(2):
                    r = ORDER[2 * h + side]
                    block = fresh[HALF * side : HALF * (side + 1)]
                    later[t, r + 1, PAD : PAD + HALF] = block
                    begin, end = block[:1], block[HALF - 1 :]
                    at = 2 * PLACED.index(t) + side
                    e2d_out[h, at : at + 1] = jnp.where(row_is0, begin, end)
                    e2p_out[h, at : at + 1] = jnp.where(row_is0, end, begin)
                    if r == ROWS - 1:
                        z2_out[0, PLACED.index(t)] = block.astype(b16)
                    if r == 0:
                        z2_out[1, PLACED.index(t)] = block.astype(b16)

    for copy in w2_loads:
        copy.wait()
    first_network(0, late)
    first_update(0, PRODUCTS[0] + PRODUCTS[1])
    e2[0][1].start()
    when(has_far, e2[0][0].start)
    for d, there, copy in ((0, has_s, zf_n), (1, has_n, zf_s)):
        @pl.when(there)
        def _(d=d, copy=copy):
            for one in copy:
                one.wait_recv()
            for t in range(OWN):
                at = (3, 4, 1, 2)[t] if d else t
                state[5 + t, 5 * d, PAD : PAD + HALF] = zf_in[d, at].astype(f32)
            state[4, 5 * d, PAD : PAD + HALF] = jnp.where(
                mine, z1_in[d, 4].astype(f32), unpack(zf_in[d, 4 - 4 * d], d, is_high)
            )
    propagate(state, range(OWN, TILES), 1, False, False)
    first_network(1, slice(TILE * 4, TILE * 9))
    first_update(1, PRODUCTS[0])
    when(has_n, z2[0][0].start)
    when(has_s, z2[0][1].start)
    first_update(1, PRODUCTS[1])
    e2[1][1].start()
    when(has_far, e2[1][0].start)
    when(has_n, z2[1][0].start)
    when(has_s, z2[1][1].start)

    def last_update(h, tiles):
        rows = halves[h]
        for _, t, fresh in update(tiles, rows):
            upper, under = fresh[:HALF], fresh[HALF:]
            if t > OWN:
                at = 2 * (t - 5)
                f_out[h, at] = upper.astype(b16)
                f_out[h, at + 1] = under.astype(b16)
            if t == OWN:
                f_out[h, 8] = pack(upper, under, is_high)
            if t <= OWN:
                done[t, rows] = fresh

    def last_sends(h):
        last_update(h, (5, 6))
        final[h][0].start()
        last_update(h, (7, 8))
        if h == 1:
            final[h][1].start()
        last_update(h, (4,))
        final[h][-1].start()

    def second_edges(h):
        e2[h][1].wait_recv()
        when(has_far, e2[h][0].wait_recv)
        for t in range(TILES):
            at = 2 * PLACED.index(mirror(t))
            lines = slice(at, at + 2)
            edges(later, t, ORDER[2 * h : 2 * h + 2], e2p_in[h, lines], e2d_in[h, lines])

    second_edges(0)
    propagate(later, range(TILES), 0, True, False)
    finish_sums(halves[0])
    for n in range(4):
        lanes = slice(256 * n, 256 * (n + 1))
        activate(n, dot(p16[halves[0]], w1[:, lanes]), halves[0])
    last_sends(0)

    second_edges(1)
    for g, tiles in enumerate(GROUPS):
        for d, there in ((0, has_s), (1, has_n)):
            @pl.when(there)
            def _(d=d, g=g, tiles=tiles):
                z2[g][d].wait_recv()
                for t in tiles:
                    later[t, 5 * d, PAD : PAD + HALF] = z2_in[d, PLACED.index(t)].astype(f32)
        propagate(later, tiles, 1, g == 0, False)
    finish_sums(halves[1])
    scale = 1.0 / (STEPS * STEPS * comps)
    packed = jnp.zeros((HALF, TILE), f32)
    for k in range(2):
        for n, r in enumerate(ORDER):
            push = sums[2 + k, HALF * n : HALF * (n + 1), :].sum(axis=1, keepdims=True)
            packed = jnp.where(lane == 4 * k + r, scale * push, packed)
    small[...] = jnp.zeros_like(small)
    small[pl.ds(half_at, HALF), :] = packed
    small_t[...] = small[...].T
    st_out[...] = small_t[0:8]
    stress_pair.start()
    when(has_n, stress_n.start, stress_on.start)
    when(has_s, stress_s.start, stress_os.start)
    for n in range(4):
        lanes = slice(256 * n, 256 * (n + 1))
        activate(n, dot(p16[halves[1]], w1[:, lanes]), halves[1])
    last_sends(1)
    for h in range(2):
        for tiles in ((0, 1), (2, 3)):
            last_update(h, tiles)
    stress_pair.wait_recv()
    st_full[...] = st_out[...] + st_in[...]

    def turn_back(h, t):
        for side in range(2):
            n = 2 * h + side
            own = done[t, HALF * n : HALF * (n + 1)]
            if t < OWN:
                came = f_in[h, 2 * t + side].astype(f32)
            else:
                came = unpack(f_in[h, 8], side, is_low)
            turned = jnp.concatenate(
                [jnp.where(half_is0, own, came), jnp.where(half_is0, came, own)], axis=0
            ).T
            r = ORDER[n]
            if t < OWN:
                out[pl.ds(me * HALF + TILE * t, TILE), r, :] = turned
            else:
                out[pl.ds(other * (comps - HALF), HALF), r, :] = jnp.where(
                    half_is0, turned[:HALF], turned[HALF:]
                )

    final[0][0].wait_recv()
    for t in (0, 1):
        turn_back(0, t)
    final[0][1].wait_recv()
    for t in (2, 3, 4):
        turn_back(0, t)

    sb_load.wait()
    srows_load.wait()
    when(has_s, stress_n.wait_recv, stress_on.wait_recv)
    when(has_n, stress_s.wait_recv, stress_os.wait_recv)
    beyond = [sz_in[d] + sx_in[d] for d in range(2)]
    for k in range(2):
        lines = [beyond[0][4 * k + 3 : 4 * k + 4]]
        lines += [st_full[4 * k + r : 4 * k + r + 1] for r in range(ROWS)]
        lines += [beyond[1][4 * k : 4 * k + 1]]
        for r in range(ROWS):
            total = sb[r, 0] * choose(srows, r, 0, *lines[r : r + 3])
            total = total + sb[r, 1] * choose(srows, r, 1, *lines[r : r + 3])
            stress = total.T.sum(axis=0, keepdims=True)
            wet = msk[r : r + 1, :].astype(f32)
            at = 16 * k
            o_out[at : at + 1, r, :] = o_out[at : at + 1, r, :] + wet * (STRESS_GAIN * stress)

    for n, tiles in enumerate(((0, 1), (2, 3), (4,))):
        final[1][n].wait_recv()
        for t in tiles:
            turn_back(1, t)

    when(has_n, ocean_n.wait_send, z1_n.wait_send, stress_n.wait_send, stress_on.wait_send)
    when(has_s, ocean_s.wait_send, z1_s.wait_send, stress_s.wait_send, stress_os.wait_send)
    for n in range(2):
        when(has_n, zf_n[n].wait_send)
        when(has_s, zf_s[n].wait_send)
    when(has_e, ocean_e.wait_send)
    when(has_w, ocean_w.wait_send)
    when(has_same, e_same.wait_send)
    when(has_far, e_diag.wait_send)
    for copy in swap[0] + swap[1] + [e_pair, stress_pair] + final[0] + final[1]:
        copy.wait_send()
    for g in range(len(GROUPS)):
        when(has_n, z2[g][0].wait_send)
        when(has_s, z2[g][1].wait_send)
    for h in range(2):
        when(has_far, e2[h][0].wait_send)
        e2[h][1].wait_send()


def kernel_call(
    spectra, first, second, table, ocean, wind, mask, cblocks, sblocks, crows, srows
):
    f32, b16 = jnp.float32, jnp.bfloat16
    comps = spectra.shape[0]
    units = first.shape[1]
    total = TILE * TILES
    shape = jax.ShapeDtypeStruct
    dma = pltpu.SemaphoreType.DMA
    groups = len(GROUPS)
    vmem = pltpu.VMEM
    scratch = [
        vmem((comps + 2 * HALF, ROWS, COLS), f32),
        vmem((total, units), b16),
        vmem((units, total), b16),
        vmem((TILES, 8, TILE), f32),
        vmem(ocean.shape, f32),
        vmem(wind.shape, f32),
        vmem(mask.shape, jnp.int32),
        vmem((ROWS, 2, HALF, COLS), f32),
        vmem((ROWS, 2, COLS, COLS), f32),
        vmem((TILES, ROWS + 2, HALF + 2 * PAD, TILE), f32),
        vmem((TILES, ROWS + 2, HALF + 2 * PAD, TILE), f32),
        vmem((TILES, CELLS, TILE), f32),
        vmem((TILES, CELLS, TILE), f32),
        vmem((CELLS, total), b16),
        vmem((CELLS, units), f32),
        vmem((CELLS, units), b16),
        vmem((4, CELLS, TILE), f32),
        vmem((5, CELLS, TILE), f32),
        vmem((CELLS, TILE), f32),
        vmem((CELLS, TILE), f32),
        vmem((CELLS, TILE), f32),
        vmem((TILE, TILE), f32),
        vmem((TILE, TILE), f32),
        vmem((2, TILES, HALF, TILE), b16),
        vmem((2, TILES, HALF, TILE), b16),
        vmem((2, OWN + 1, HALF, TILE), b16),
        vmem((2, OWN + 1, HALF, TILE), b16),
        vmem((2, OWN + 1, HALF, TILE), b16),
        *[vmem((24, TILE), f32) for _ in range(7)],
        vmem((2, TILES, HALF, TILE), b16),
        vmem((2, TILES, HALF, TILE), b16),
        *[vmem((2, 24, TILE), f32) for _ in range(4)],
        vmem((2, 64, COLS), f32),
        vmem((2, 64, COLS), f32),
        vmem((256, COLS), f32),
        vmem((COLS, 256), f32),
        vmem((2, COLS, 256), f32),
        vmem((8, COLS), f32),
        vmem((8, COLS), f32),
        vmem((8, COLS), f32),
        vmem((2, 8, COLS), f32),
        vmem((2, 8, COLS), f32),
        vmem((2, TILES, HALF, TILE), b16),
        vmem((2, TILES, HALF, TILE), b16),
        vmem((OWN + 1, CELLS, TILE), f32),
        pltpu.SMEM((2, 1, ROWS), jnp.int32),
        pltpu.SMEM((2, 1, ROWS), jnp.int32),
        dma((15,)),
        dma((2,)), dma((2,)),
        dma((2,)), dma((2,)),
        dma((2, 4)), dma((2, 4)),
        dma((2,)), dma((2,)),
        dma((2, 2)), dma((2, 2)),
        dma((3,)), dma((3,)),
        dma((2, groups)), dma((2, groups)),
        dma((2, groups)), dma((2, groups)),
        dma((5,)), dma((5,)),
        dma((2, 3)), dma((2, 3)),
    ]
    return pl.pallas_call(
        kernel,
        out_shape=(shape(spectra.shape, f32), shape(ocean.shape, f32)),
        in_specs=[pl.BlockSpec(memory_space=pl.ANY)] * 11,
        out_specs=(pl.BlockSpec(memory_space=pltpu.VMEM),) * 2,
        scratch_shapes=scratch,
        compiler_params=pltpu.CompilerParams(
            vmem_limit_bytes=VMEM_LIMIT, collective_id=0, has_side_effects=True
        ),
    )(*(
        pltpu.with_memory_space_constraint(x, pltpu.HBM)
        for x in (
            spectra, first, second, table, ocean, wind, mask, cblocks, sblocks, crows, srows
        )
    ))


PIECES = 4


def place_kernel(a, b, a_out, b_out, sems):
    rows = a.shape[0] // PIECES
    copies = [pltpu.make_async_copy(b, b_out, sems.at[PIECES])]
    for n in range(PIECES):
        part = pl.ds(n * rows, rows)
        copies.append(pltpu.make_async_copy(a.at[part], a_out.at[part], sems.at[n]))
    for copy in copies:
        copy.start()
    for copy in copies:
        copy.wait()


def place_call(a, b):
    shape = jax.ShapeDtypeStruct
    return pl.pallas_call(
        place_kernel,
        out_shape=(shape(a.shape, a.dtype), shape(b.shape, b.dtype)),
        in_specs=[pl.BlockSpec(memory_space=pl.ANY)] * 2,
        out_specs=(pl.BlockSpec(memory_space=pl.ANY),) * 2,
        scratch_shapes=[pltpu.SemaphoreType.DMA((PIECES + 1,))],
        compiler_params=pltpu.CompilerParams(vmem_limit_bytes=VMEM_LIMIT),
    )(a, b)


def local_step(
    spectra,
    wind_field,
    sea_mask,
    first_layer,
    second_layer,
    ocean_state,
    current_blocks,
    current_rows,
    stress_blocks,
    stress_rows,
):
    half_freqs, directions, rows, cols = spectra.shape
    variables, levels = ocean_state.shape[:2]
    table = jnp.asarray(tables(2 * half_freqs, directions))
    state, ocean = kernel_call(
        spectra.reshape(half_freqs * directions, rows, cols),
        first_layer,
        second_layer,
        table,
        ocean_state.reshape(variables * levels, rows, cols),
        wind_field,
        sea_mask,
        current_blocks,
        stress_blocks,
        current_rows.transpose(1, 2, 0),
        stress_rows.transpose(1, 2, 0),
    )
    state, ocean = place_call(state, ocean)
    return state.reshape(spectra.shape), ocean.reshape(ocean_state.shape)


def solution(mesh):
    placed = (
        P("comp", None, "gy", "gx"),
        P(None, "gy", "gx"),
        P("gy", "gx"),
        P(),
        P(),
        P(None, None, "gy", "gx"),
        P("gy", None, "gx", None),
        P("gy", None, "gx"),
        P("gy", None, "gx", None),
        P("gy", None, "gx"),
    )
    return jax.shard_map(
        local_step,
        mesh=mesh,
        in_specs=placed,
        out_specs=(P("comp", None, "gy", "gx"), P(None, None, "gy", "gx")),
        check_vma=False,
    )
```

```python
import numpy as np

import jax
import jax.numpy as jnp
from jax import lax
from jax.experimental import pallas as pl
from jax.experimental.pallas import tpu as pltpu
from jax.sharding import PartitionSpec as P

CURRENT_GAIN = 0.08
WIND_GAIN = 0.06
DECAY_GAIN = 0.03
NONLINEAR_GAIN = 0.3
THERMAL = 0.2
HALINE = 0.8
CORIOLIS = 0.1
PRESSURE_GAIN = 0.2
LATERAL_MIX = 0.1
VERTICAL_MIX = 0.2
ADVECTION = 0.3
STRESS_GAIN = 150.0

STEPS = 2
ROWS = 4
COLS = 128
HALF = 64
CELLS = ROWS * HALF
TILE = 128
TILES = 9
OWN = 4
PAD = 8
GROUPS = ((0, 1, 5, 6), (2, 3, 7, 8, 4))
PLACED = GROUPS[0] + GROUPS[1]
PRODUCTS = (((0, 1), (5, 6)), ((2, 3), (7, 8), (4,)))
SWAP_SLOTS = (
    (pl.ds(0, 2), pl.ds(7, 2), pl.ds(2, 3), pl.ds(5, 2)),
    (pl.ds(0, 5), pl.ds(5, 4)),
)
NORTH_SLOTS = ((pl.ds(0, 2), pl.ds(0, 2)), (pl.ds(2, 3), pl.ds(2, 3)))
SOUTH_SLOTS = ((pl.ds(7, 2), pl.ds(3, 2)), (pl.ds(4, 3), pl.ds(0, 3)))
ORDER = (1, 2, 0, 3)
SWAPPED = ((3, 0), (1, 2))
FINAL = (((0, 4), (4, 9)), ((0, 4), (4, 8), (8, 9)))
VMEM_LIMIT = 32 * 1024 * 1024


def tables(total, directions):
    index = np.arange(total, dtype=np.float64)
    group = 0.4 * np.exp(-3.0 * index / (total - 1))
    ratio = np.exp(2.0 * index / (total - 1) - 1.0)
    angles = 2.0 * np.pi * np.arange(directions) / directions
    cosines, sines = np.cos(angles), np.sin(angles)
    full = np.zeros((8, total, directions))
    full[0] = group[:, None] * cosines
    full[1] = group[:, None] * sines
    full[2] = cosines
    full[3] = sines
    full[4] = WIND_GAIN * 4.0 * group[:, None]
    full[5] = ratio[:, None]
    tiled = full.reshape(8, TILES, TILE).transpose(1, 0, 2)
    swapped = np.concatenate([tiled[5:], tiled[4:5], tiled[:4]])
    return np.stack([tiled, swapped]).astype(np.float32)


def mirror(t):
    return 4 if t == 4 else (t + 5) % 10


def kernel(
    spectra, first, second, table, ocean, wind, mask, cblocks, sblocks, crows_in, srows_in,
    out, o_out,
    spec, w1, w2, tab, oc, wnd, msk, cb, sb,
    state, later, prop, rate, p16, part, hidden, sums, cells, gain, back, squared, small, small_t,
    y_out, y_in, z1_out, z1_in, zf_in, es_out, es_in, ed_out, ed_in, ep_out, ep_in, el,
    z2_out, z2_in, e2d_out, e2d_in, e2p_out, e2p_in,
    oz_out, oz_in, ocat, ox_out, ox_in, st_out, st_in, st_full, sz_in, sx_in, f_out, f_in, done,
    crows, srows, load, oz_send, oz_recv, ox_send, ox_recv, y_send, y_recv, z1_send, z1_recv,
    zf_send, zf_recv, e1_send, e1_recv, z2_send, z2_recv, e2_send, e2_recv,
    s_send, s_recv, f_send, f_recv,
):
    f32, b16 = jnp.float32, jnp.bfloat16
    me = lax.axis_index("comp")
    other = 1 - me
    gy, ny = lax.axis_index("gy"), lax.axis_size("gy")
    gx, nx = lax.axis_index("gx"), lax.axis_size("gx")
    comps = spectra.shape[0]
    mesh_ids = pl.DeviceIdType.MESH

    def local(source, target, n):
        return pltpu.make_async_copy(source, target, load.at[n])

    own_at = pl.multiple_of(me * 5 * TILE, TILE)
    far_at = pl.multiple_of(other * 5 * TILE, TILE)
    half_at = pl.multiple_of(me * HALF, HALF)
    cut = HALF + 2 * TILE
    spec_load = local(spectra.at[pl.ds(0, cut)], spec.at[pl.ds(HALF, cut)], 0)
    spec_rest = local(
        spectra.at[pl.ds(cut, comps - cut)], spec.at[pl.ds(HALF + cut, comps - cut)], 15
    )
    ocean_load = local(ocean, oc, 1)
    wind_load = local(wind, wnd, 2)
    mask_load = local(mask, msk, 3)
    table_load = local(table.at[me], tab, 4)
    cb_load = local(cblocks.at[:, :, pl.ds(half_at, HALF), :], cb, 5)
    sb_load = local(sblocks, sb, 6)
    w1_loads = [
        local(first.at[pl.ds(own_at, 512)], w1.at[pl.ds(0, 512)], 7),
        local(first.at[pl.ds(512, 128)], w1.at[pl.ds(512, 128)], 8),
        local(first.at[pl.ds(far_at, 512)], w1.at[pl.ds(640, 512)], 9),
    ]
    w2_loads = [
        local(second.at[:, pl.ds(own_at, 512)], w2.at[:, pl.ds(0, 512)], 10),
        local(second.at[:, pl.ds(512, 128)], w2.at[:, pl.ds(512, 128)], 11),
        local(second.at[:, pl.ds(far_at, 512)], w2.at[:, pl.ds(640, 512)], 12),
    ]
    crows_load = local(crows_in, crows, 13)
    srows_load = local(srows_in, srows, 14)
    for copy in (spec_load, spec_rest, ocean_load, wind_load, mask_load, table_load, crows_load):
        copy.start()

    for ref in (es_in, ed_in, e2d_in, sz_in, sx_in, ox_in, oz_in):
        ref[...] = jnp.zeros_like(ref)

    has_s, has_n = gy > 0, gy < ny - 1
    has_w, has_e = gx > 0, gx < nx - 1
    south = {"gy": lax.rem(gy + ny - 1, ny)}
    north = {"gy": lax.rem(gy + 1, ny)}
    west = {"gx": lax.rem(gx + nx - 1, nx)}
    east = {"gx": lax.rem(gx + 1, nx)}
    pair = {"comp": other}
    far_gx = gx + 2 * me - 1
    has_far = jnp.logical_and(far_gx >= 0, far_gx < nx)
    diag = {"comp": other, "gx": lax.rem(far_gx + nx, nx)}
    same_gx = gx + 1 - 2 * me
    has_same = jnp.logical_and(same_gx >= 0, same_gx < nx)
    same = {"gx": lax.rem(same_gx + nx, nx)}

    barrier = pltpu.get_barrier_semaphore()
    greet = ((has_s, south), (has_n, north), (has_w, west), (has_e, east), (has_far, diag))
    other_n, other_s = {**pair, **north}, {**pair, **south}
    greet += ((has_n, other_n), (has_s, other_s))
    for there, place in greet:
        @pl.when(there)
        def _(place=place):
            pl.semaphore_signal(barrier, inc=1, device_id=place, device_id_type=mesh_ids)
    pl.semaphore_signal(barrier, inc=1, device_id=pair, device_id_type=mesh_ids)

    def remote(source, target, send, recv, where):
        return pltpu.make_async_remote_copy(
            src_ref=source, dst_ref=target, send_sem=send, recv_sem=recv,
            device_id=where, device_id_type=mesh_ids,
        )

    ocean_n = remote(oz_out.at[0], oz_in.at[0], oz_send.at[0], oz_recv.at[0], north)
    ocean_s = remote(oz_out.at[1], oz_in.at[1], oz_send.at[1], oz_recv.at[1], south)
    ocean_e = remote(
        ox_out.at[pl.ds(120, 8)], ox_in.at[0, pl.ds(120, 8)], ox_send.at[0], ox_recv.at[0], east
    )
    ocean_w = remote(
        ox_out.at[pl.ds(0, 8)], ox_in.at[1, pl.ds(0, 8)], ox_send.at[1], ox_recv.at[1], west
    )
    swap = [
        [
            remote(
                y_out.at[p, part_of], y_in.at[p, part_of], y_send.at[p, n], y_recv.at[p, n], pair
            )
            for n, part_of in enumerate(SWAP_SLOTS[p])
        ]
        for p in range(2)
    ]
    z1_n = remote(z1_out.at[0], z1_in.at[0], z1_send.at[0], z1_recv.at[0], north)
    z1_s = remote(z1_out.at[1], z1_in.at[1], z1_send.at[1], z1_recv.at[1], south)
    zf_n = [
        remote(y_in.at[0, a], zf_in.at[0, b], zf_send.at[0, n], zf_recv.at[0, n], north)
        for n, (a, b) in enumerate(NORTH_SLOTS)
    ]
    zf_s = [
        remote(y_in.at[0, a], zf_in.at[1, b], zf_send.at[1, n], zf_recv.at[1, n], south)
        for n, (a, b) in enumerate(SOUTH_SLOTS)
    ]
    e_same = remote(es_out, es_in, e1_send.at[0], e1_recv.at[0], same)
    e_diag = remote(ed_out, ed_in, e1_send.at[1], e1_recv.at[1], diag)
    e_pair = remote(ep_out, ep_in, e1_send.at[2], e1_recv.at[2], pair)

    z2 = []
    e2 = []
    for g, tiles in enumerate(GROUPS):
        part_of = pl.ds(PLACED.index(tiles[0]), len(tiles))
        z2.append([
            remote(
                z2_out.at[d, part_of], z2_in.at[d, part_of],
                z2_send.at[d, g], z2_recv.at[d, g], (north, south)[d],
            )
            for d in range(2)
        ])

    for h in range(2):
        e2.append([
            remote(e2d_out.at[h], e2d_in.at[h], e2_send.at[0, h], e2_recv.at[0, h], diag),
            remote(e2p_out.at[h], e2p_in.at[h], e2_send.at[1, h], e2_recv.at[1, h], pair),
        ])
    stress_pair = remote(st_out, st_in, s_send.at[0], s_recv.at[0], pair)
    stress_n = remote(st_out, sz_in.at[0], s_send.at[1], s_recv.at[1], north)
    stress_s = remote(st_out, sz_in.at[1], s_send.at[2], s_recv.at[2], south)
    stress_on = remote(st_out, sx_in.at[0], s_send.at[3], s_recv.at[3], other_n)
    stress_os = remote(st_out, sx_in.at[1], s_send.at[4], s_recv.at[4], other_s)
    final = []
    for h in range(2):
        final.append([])
        for n, (begin, end) in enumerate(FINAL[h]):
            slots = pl.ds(begin, end - begin)
            final[h].append(
                remote(
                    f_out.at[h, slots], f_in.at[h, slots], f_send.at[h, n], f_recv.at[h, n], pair
                )
            )

    def when(condition, *actions):
        @pl.when(condition)
        def _():
            for action in actions:
                action()

    for edge in (0, ROWS + 1):
        for field in (state, later):
            field[:, edge, PAD : PAD + HALF] = jnp.zeros((TILES, HALF, TILE), f32)
    spec[:HALF] = jnp.zeros((HALF, ROWS, COLS), f32)
    spec[HALF + comps :] = jnp.zeros((HALF, ROWS, COLS), f32)

    half_is0 = jnp.broadcast_to(me, (HALF, TILE)) == 0
    row_is0 = jnp.broadcast_to(me, (1, TILE)) == 0
    lane = lax.broadcasted_iota(jnp.int32, (HALF, TILE), 1)
    mine = jnp.where(lane < 64, 0, 1) == me

    def pack(first_row, second_row, low_lanes):
        left = jnp.where(low_lanes, first_row, pltpu.roll(first_row, 64, 1))
        right = jnp.where(low_lanes, pltpu.roll(second_row, 64, 1), second_row)
        return jnp.where(lane < 64, left, right).astype(b16)

    def unpack(packed, side, low_lanes):
        wide = packed.astype(f32)
        turned = pltpu.roll(wide, 64, 1)
        if side == 0:
            return jnp.where(low_lanes, wide, turned)
        return jnp.where(low_lanes, turned, wide)

    is_low, is_high = half_is0, jnp.logical_not(half_is0)
    starts = [HALF + me * HALF + TILE * t for t in range(OWN)] + [other * (comps + HALF - 64)]
    spec_load.wait()
    counted = [jnp.where(there, 1, 0) for there, _ in greet]

    def y_slot(p, side, t):
        if p == 0:
            return (7, 8, 5, 6)[t] if side else t
        return 1 + 2 * t + side

    def turn(p, side, t):
        r = SWAPPED[p][side]
        turned = spec[pl.ds(starts[t], TILE), r, :].T
        low, high = turned[:HALF], turned[HALF:]
        own = jnp.where(half_is0, low, high)
        far = jnp.where(half_is0, high, low)
        state[t, r + 1, PAD : PAD + HALF] = own
        if t < OWN:
            y_out[p, y_slot(p, side, t)] = far.astype(b16)
        if r == 3:
            z1_out[0, t] = own.astype(b16)
        if r == 0:
            z1_out[1, t] = own.astype(b16)
        at = 4 * t + r
        es_out[at : at + 1] = jnp.where(row_is0, turned[127:128], turned[0:1])
        ed_out[at : at + 1] = jnp.where(row_is0, turned[0:1], turned[127:128])
        ep_out[at : at + 1] = jnp.where(row_is0, turned[63:64], turned[64:65])
        el[at : at + 1] = jnp.where(row_is0, turned[64:65], turned[63:64])
        return far

    for side in range(2):
        for t in (0, 1):
            turn(0, side, t)
        if side == 0:
            pl.semaphore_wait(barrier, 1 + sum(counted))
        swap[0][side].start()
    spec_rest.wait()
    for copy in [cb_load] + w1_loads + w2_loads + [sb_load, srows_load]:
        copy.start()
    for side in range(2):
        for t in (2, 3):
            turn(0, side, t)
    y_out[0, 4] = pack(turn(0, 0, 4), turn(0, 1, 4), is_low)
    swap[0][2].start()
    swap[0][3].start()
    when(has_n, z1_n.start)
    when(has_s, z1_s.start)
    for t in range(OWN):
        for side in range(2):
            turn(1, side, t)
    y_out[1, 0] = pack(turn(1, 0, 4), turn(1, 1, 4), is_low)
    swap[1][0].start()
    when(has_far, e_diag.start)
    e_pair.start()
    swap[1][1].start()
    when(has_same, e_same.start)

    ocean_load.wait()
    oz_out[0] = oc[:, ROWS - 1, :]
    oz_out[1] = oc[:, 0, :]
    when(has_n, ocean_n.start)
    when(has_s, ocean_s.start)
    for r in range(ROWS):
        ocat[64 * r : 64 * (r + 1), :] = oc[:, r, :]
    ox_out[...] = ocat[...].T
    when(has_e, ocean_e.start)
    when(has_w, ocean_w.start)

    wind_load.wait()
    mask_load.wait()
    table_load.wait()
    small[...] = jnp.zeros_like(small)
    small[0:4] = msk[...].astype(f32)
    small[4:8] = WIND_GAIN * wnd[0]
    small[8:12] = WIND_GAIN * wnd[1]
    small_t[...] = small[...].T
    columns = small_t[pl.ds(half_at, HALF), :]
    for q in range(3):
        for r in range(ROWS):
            n = 4 * q + r
            at = HALF * ORDER.index(r)
            cells[2 + q, at : at + HALF, :] = jnp.broadcast_to(
                columns[:, n : n + 1], (HALF, TILE)
            )
    cb_load.wait()
    crows_load.wait()
    when(has_s, ocean_n.wait_recv)
    when(has_n, ocean_s.wait_recv)

    def choose(rows_ref, r, b, below, here, above):
        offset = jnp.broadcast_to(rows_ref[b, 0, r] - gy * ROWS - r, (1, COLS))
        return jnp.where(offset < 0, below, jnp.where(offset == 0, here, above))

    for k in range(2):
        at = 16 * k
        lines = [oz_in[0, at : at + 1]]
        lines += [oc[at : at + 1, r, :] for r in range(ROWS)]
        lines += [oz_in[1, at : at + 1]]
        for r in range(ROWS):
            total = cb[r, 0] * choose(crows, r, 0, *lines[r : r + 3])
            total = total + cb[r, 1] * choose(crows, r, 1, *lines[r : r + 3])
            place = HALF * ORDER.index(r)
            cells[k, place : place + HALF, :] = jnp.broadcast_to(
                CURRENT_GAIN * total.sum(axis=1, keepdims=True), (HALF, TILE)
            )

    def edges(field, t, rows, pair_side, far_side):
        for n, r in enumerate(rows):
            near, away = pair_side[n : n + 1], far_side[n : n + 1]
            field[t, r + 1, PAD - 1 : PAD] = jnp.where(row_is0, away, near)
            field[t, r + 1, PAD + HALF : PAD + HALF + 1] = jnp.where(row_is0, near, away)

    def propagate(field, tiles, h, fresh, fresh_push):
        def body(i, carry):
            at = pl.multiple_of((2 * h + i) * HALF, HALF)
            r = 3 * i if h else 1 + i
            for lo in (0, 32):
                cell = pl.ds(at + lo, 32)
                cur_x, cur_y, wet, wind_x, wind_y = (cells[q, cell, :] for q in range(5))
                zero = jnp.zeros((32, TILE), f32)
                totals = [
                    zero if (fresh if q < 2 else fresh_push) else sums[q, cell, :]
                    for q in range(4)
                ]
                for t in tiles:
                    speed_x, speed_y, cos, sin, phase, ratio = (
                        tab[t, q : q + 1, :] for q in range(6)
                    )
                    top = PAD + lo
                    here = field[t, r + 1, top : top + 32]
                    before = field[t, r + 1, top - 1 : top + 31]
                    after = field[t, r + 1, top + 1 : top + 33]
                    below = field[t, r, top : top + 32]
                    above = field[t, r + 2, top : top + 32]
                    cx = speed_x + cur_x
                    cy = speed_y + cur_y
                    flux = jnp.abs(cx) * (here - jnp.where(cx > 0.0, before, after))
                    flux = flux + jnp.abs(cy) * (here - jnp.where(cy > 0.0, below, above))
                    moved = wet * (here - flux)
                    growth = jnp.maximum(wind_x * cos + wind_y * sin - phase, 0.0)
                    pushed = growth * moved
                    prop[t, cell, :] = moved
                    rate[t, cell, :] = growth
                    p16[cell, TILE * t : TILE * (t + 1)] = moved.astype(b16)
                    parts = (moved, ratio * moved, pushed * cos, pushed * sin)
                    totals = [a + b for a, b in zip(totals, parts)]
                for q in range(4):
                    sums[q, cell, :] = totals[q]
            return carry

        lax.fori_loop(0, 2, body, 0, unroll=True)

    def finish_sums(rows):
        total = STEPS * comps
        count = rows.stop - rows.start

        def spread(n):
            return jnp.broadcast_to(
                sums[n, rows, :].sum(axis=1, keepdims=True), (count, TILE)
            )

        floor = jnp.maximum(spread(0), 1.0)
        share = spread(1) / floor
        squared[rows] = DECAY_GAIN * share * share
        gain[rows] = (0.5 * total) / floor
        back[rows] = (NONLINEAR_GAIN / total) * floor

    def dot(left, right):
        return lax.dot_general(
            left, right, (((1,), (0,)), ((), ())), preferred_element_type=f32
        )

    def activate(n, pre, rows):
        for j in range(2):
            half = pre[:, TILE * j : TILE * (j + 1)] * gain[rows]
            at = 256 * n + TILE * j
            hidden[rows, at : at + TILE] = (half + half * jnp.tanh(half)).astype(b16)

    def update(tiles, rows):
        at = TILE * tiles[0]
        moved = dot(hidden[rows], w2[:, at : at + TILE * len(tiles)])
        for j, t in enumerate(tiles):
            transfer = moved[:, TILE * j : TILE * (j + 1)].astype(b16).astype(f32)
            fresh = prop[t, rows] * jnp.exp(rate[t, rows] - tab[t, 5:6, :] * squared[rows])
            yield j, t, fresh + back[rows] * transfer

    whole = slice(0, CELLS)
    halves = (slice(0, CELLS // 2), slice(CELLS // 2, CELLS))

    swap[0][0].wait_recv()
    when(has_n, zf_n[0].start)
    swap[0][1].wait_recv()
    when(has_s, zf_s[0].start)
    when(has_s, z1_n.wait_recv)
    when(has_n, z1_s.wait_recv)
    when(has_far, e_same.wait_recv)
    for t in range(OWN):
        edges(state, t, range(4), el[4 * t : 4 * t + 4], es_in[4 * t : 4 * t + 4])
    for d, there in ((0, has_s), (1, has_n)):
        @pl.when(there)
        def _(d=d):
            for t in range(OWN):
                state[t, 5 * d, PAD : PAD + HALF] = z1_in[d, t].astype(f32)
    for h in range(2):
        propagate(state, range(OWN), h, True, True)
    swap[0][2].wait_recv()
    when(has_n, zf_n[1].start)
    swap[0][3].wait_recv()
    when(has_s, zf_s[1].start)
    for copy in w1_loads:
        copy.wait()
    for n in range(4):
        lanes = slice(256 * n, 256 * (n + 1))
        part[:, lanes] = dot(p16[:, : TILE * OWN], w1[: TILE * OWN, lanes])

    when(has_w, ocean_e.wait_recv)
    when(has_e, ocean_w.wait_recv)
    from_w, from_e = ox_in[0].T, ox_in[1].T
    lane64 = lax.broadcasted_iota(jnp.int32, (64, COLS), 1)
    level64 = lax.rem(lax.broadcasted_iota(jnp.int32, (64, COLS), 0), 16)
    level = lax.broadcasted_iota(jnp.int32, (16, COLS), 0)

    def density(field):
        return HALINE * field[48:64] - THERMAL * field[32:48]

    def pressure(dense):
        running = dense
        for shift in (1, 2, 4, 8):
            running = running + jnp.where(level >= shift, pltpu.roll(running, shift, 0), 0.0)
        return running - 0.5 * dense

    for r in range(ROWS):
        here = oc[:, r, :]
        low = oz_in[0] if r == 0 else oc[:, r - 1, :]
        high = oz_in[1] if r == ROWS - 1 else oc[:, r + 1, :]
        lines = slice(64 * r, 64 * (r + 1))
        left = pltpu.roll(jnp.where(lane64 == COLS - 1, from_w[lines], here), 1, 1)
        right = pltpu.roll(jnp.where(lane64 == 0, from_e[lines], here), COLS - 1, 1)
        upper = jnp.where(level64 == 0, here, pltpu.roll(here, 1, 0))
        lower = jnp.where(level64 == 15, here, pltpu.roll(here, 63, 0))
        mixed = LATERAL_MIX * (left + right + low + high - 4.0 * here)
        mixed = mixed + VERTICAL_MIX * (upper + lower - 2.0 * here)
        across, along = right - left, high - low
        speed_u, speed_v = here[0:16], here[16:32]
        half_gain = 0.5 * PRESSURE_GAIN
        du = CORIOLIS * speed_v - half_gain * pressure(density(across))
        dv = -CORIOLIS * speed_u - half_gain * pressure(density(along))
        pull = -0.5 * ADVECTION
        dtemp = pull * (speed_u * across[32:48] + speed_v * along[32:48])
        dsalt = pull * (speed_u * across[48:64] + speed_v * along[48:64])
        tendency = mixed + jnp.concatenate([du, dv, dtemp, dsalt], axis=0)
        o_out[:, r, :] = here + msk[r : r + 1, :].astype(f32) * tendency


    def merge(p, side, r):
        packed = y_in[p, 4 if p == 0 else 0]
        state[4, r + 1, PAD : PAD + HALF] = jnp.where(
            mine, state[4, r + 1, PAD : PAD + HALF], unpack(packed, side, is_high)
        )

    def arrived(p, side, r, t):
        state[5 + t, r + 1, PAD : PAD + HALF] = y_in[p, y_slot(p, side, t)].astype(f32)

    for side, r in enumerate(SWAPPED[0]):
        for t in range(OWN):
            arrived(0, side, r, t)
        merge(0, side, r)
    swap[1][0].wait_recv()
    when(has_far, e_diag.wait_recv)
    e_pair.wait_recv()
    for t in range(OWN):
        lines = slice(4 * t, 4 * t + 4)
        edges(state, 5 + t, range(4), ep_in[lines], ed_in[lines])
    edges(
        state,
        4,
        range(4),
        jnp.where(mine[:4], el[16:20], ep_in[16:20]),
        jnp.where(mine[:4], es_in[16:20], ed_in[16:20]),
    )
    for side, r in enumerate(SWAPPED[1]):
        for t in (0, 1):
            arrived(1, side, r, t)
        merge(1, side, r)
    propagate(state, (4, 5, 6), 0, False, False)
    early = slice(TILE * 4, TILE * 7)
    late = slice(TILE * 7, TILE * 9)
    for n in range(4):
        lanes = slice(256 * n, 256 * (n + 1))
        extra = dot(p16[halves[0], early], w1[early, lanes])
        part[halves[0], lanes] = part[halves[0], lanes] + extra
    swap[1][1].wait_recv()
    for side, r in enumerate(SWAPPED[1]):
        for t in (2, 3):
            arrived(1, side, r, t)
    propagate(state, (7, 8), 0, False, False)

    def first_network(h, taken):
        rows = halves[h]
        finish_sums(rows)
        for n in range(4):
            lanes = slice(256 * n, 256 * (n + 1))
            activate(n, part[rows, lanes] + dot(p16[rows, taken], w1[taken, lanes]), rows)

    def first_update(h, products):
        for tiles in products:
            for _, t, fresh in update(tiles, halves[h]):
                for side in range(2):
                    r = ORDER[2 * h + side]
                    block = fresh[HALF * side : HALF * (side + 1)]
                    later[t, r + 1, PAD : PAD + HALF] = block
                    begin, end = block[:1], block[HALF - 1 :]
                    at = 2 * PLACED.index(t) + side
                    e2d_out[h, at : at + 1] = jnp.where(row_is0, begin, end)
                    e2p_out[h, at : at + 1] = jnp.where(row_is0, end, begin)
                    if r == ROWS - 1:
                        z2_out[0, PLACED.index(t)] = block.astype(b16)
                    if r == 0:
                        z2_out[1, PLACED.index(t)] = block.astype(b16)

    for copy in w2_loads:
        copy.wait()
    first_network(0, late)
    first_update(0, PRODUCTS[0] + PRODUCTS[1])
    e2[0][1].start()
    when(has_far, e2[0][0].start)
    for d, there, copy in ((0, has_s, zf_n), (1, has_n, zf_s)):
        @pl.when(there)
        def _(d=d, copy=copy):
            for one in copy:
                one.wait_recv()
            for t in range(OWN):
                at = (3, 4, 1, 2)[t] if d else t
                state[5 + t, 5 * d, PAD : PAD + HALF] = zf_in[d, at].astype(f32)
            state[4, 5 * d, PAD : PAD + HALF] = jnp.where(
                mine, z1_in[d, 4].astype(f32), unpack(zf_in[d, 4 - 4 * d], d, is_high)
            )
    propagate(state, range(OWN, TILES), 1, False, False)
    first_network(1, slice(TILE * 4, TILE * 9))
    first_update(1, PRODUCTS[0])
    when(has_n, z2[0][0].start)
    when(has_s, z2[0][1].start)
    first_update(1, PRODUCTS[1])
    e2[1][1].start()
    when(has_far, e2[1][0].start)
    when(has_n, z2[1][0].start)
    when(has_s, z2[1][1].start)

    def last_update(h, tiles):
        rows = halves[h]
        for _, t, fresh in update(tiles, rows):
            upper, under = fresh[:HALF], fresh[HALF:]
            if t > OWN:
                at = 2 * (t - 5)
                f_out[h, at] = upper.astype(b16)
                f_out[h, at + 1] = under.astype(b16)
            if t == OWN:
                f_out[h, 8] = pack(upper, under, is_high)
            if t <= OWN:
                done[t, rows] = fresh

    def last_sends(h):
        last_update(h, (5, 6))
        final[h][0].start()
        last_update(h, (7, 8))
        if h == 1:
            final[h][1].start()
        last_update(h, (4,))
        final[h][-1].start()

    def second_edges(h):
        e2[h][1].wait_recv()
        when(has_far, e2[h][0].wait_recv)
        for t in range(TILES):
            at = 2 * PLACED.index(mirror(t))
            lines = slice(at, at + 2)
            edges(later, t, ORDER[2 * h : 2 * h + 2], e2p_in[h, lines], e2d_in[h, lines])

    second_edges(0)
    propagate(later, range(TILES), 0, True, False)
    finish_sums(halves[0])
    for n in range(4):
        lanes = slice(256 * n, 256 * (n + 1))
        activate(n, dot(p16[halves[0]], w1[:, lanes]), halves[0])
    last_sends(0)

    second_edges(1)
    for g, tiles in enumerate(GROUPS):
        for d, there in ((0, has_s), (1, has_n)):
            @pl.when(there)
            def _(d=d, g=g, tiles=tiles):
                z2[g][d].wait_recv()
                for t in tiles:
                    later[t, 5 * d, PAD : PAD + HALF] = z2_in[d, PLACED.index(t)].astype(f32)
        propagate(later, tiles, 1, g == 0, False)
    finish_sums(halves[1])
    scale = 1.0 / (STEPS * STEPS * comps)
    packed = jnp.zeros((HALF, TILE), f32)
    for k in range(2):
        for n, r in enumerate(ORDER):
            push = sums[2 + k, HALF * n : HALF * (n + 1), :].sum(axis=1, keepdims=True)
            packed = jnp.where(lane == 4 * k + r, scale * push, packed)
    small[...] = jnp.zeros_like(small)
    small[pl.ds(half_at, HALF), :] = packed
    small_t[...] = small[...].T
    st_out[...] = small_t[0:8]
    stress_pair.start()
    when(has_n, stress_n.start, stress_on.start)
    when(has_s, stress_s.start, stress_os.start)
    for n in range(4):
        lanes = slice(256 * n, 256 * (n + 1))
        activate(n, dot(p16[halves[1]], w1[:, lanes]), halves[1])
    last_sends(1)
    for h in range(2):
        for tiles in ((0, 1), (2, 3)):
            last_update(h, tiles)
    stress_pair.wait_recv()
    st_full[...] = st_out[...] + st_in[...]

    def turn_back(h, t):
        for side in range(2):
            n = 2 * h + side
            own = done[t, HALF * n : HALF * (n + 1)]
            if t < OWN:
                came = f_in[h, 2 * t + side].astype(f32)
            else:
                came = unpack(f_in[h, 8], side, is_low)
            turned = jnp.concatenate(
                [jnp.where(half_is0, own, came), jnp.where(half_is0, came, own)], axis=0
            ).T
            r = ORDER[n]
            if t < OWN:
                out[pl.ds(me * HALF + TILE * t, TILE), r, :] = turned
            else:
                out[pl.ds(other * (comps - HALF), HALF), r, :] = jnp.where(
                    half_is0, turned[:HALF], turned[HALF:]
                )

    final[0][0].wait_recv()
    for t in (0, 1):
        turn_back(0, t)
    final[0][1].wait_recv()
    for t in (2, 3, 4):
        turn_back(0, t)

    sb_load.wait()
    srows_load.wait()
    when(has_s, stress_n.wait_recv, stress_on.wait_recv)
    when(has_n, stress_s.wait_recv, stress_os.wait_recv)
    beyond = [sz_in[d] + sx_in[d] for d in range(2)]
    for k in range(2):
        lines = [beyond[0][4 * k + 3 : 4 * k + 4]]
        lines += [st_full[4 * k + r : 4 * k + r + 1] for r in range(ROWS)]
        lines += [beyond[1][4 * k : 4 * k + 1]]
        for r in range(ROWS):
            total = sb[r, 0] * choose(srows, r, 0, *lines[r : r + 3])
            total = total + sb[r, 1] * choose(srows, r, 1, *lines[r : r + 3])
            stress = total.T.sum(axis=0, keepdims=True)
            wet = msk[r : r + 1, :].astype(f32)
            at = 16 * k
            o_out[at : at + 1, r, :] = o_out[at : at + 1, r, :] + wet * (STRESS_GAIN * stress)

    for n, tiles in enumerate(((0, 1), (2, 3), (4,))):
        final[1][n].wait_recv()
        for t in tiles:
            turn_back(1, t)

    when(has_n, ocean_n.wait_send, z1_n.wait_send, stress_n.wait_send, stress_on.wait_send)
    when(has_s, ocean_s.wait_send, z1_s.wait_send, stress_s.wait_send, stress_os.wait_send)
    for n in range(2):
        when(has_n, zf_n[n].wait_send)
        when(has_s, zf_s[n].wait_send)
    when(has_e, ocean_e.wait_send)
    when(has_w, ocean_w.wait_send)
    when(has_same, e_same.wait_send)
    when(has_far, e_diag.wait_send)
    for copy in swap[0] + swap[1] + [e_pair, stress_pair] + final[0] + final[1]:
        copy.wait_send()
    for g in range(len(GROUPS)):
        when(has_n, z2[g][0].wait_send)
        when(has_s, z2[g][1].wait_send)
    for h in range(2):
        when(has_far, e2[h][0].wait_send)
        e2[h][1].wait_send()


def kernel_call(
    spectra, first, second, table, ocean, wind, mask, cblocks, sblocks, crows, srows
):
    f32, b16 = jnp.float32, jnp.bfloat16
    comps = spectra.shape[0]
    units = first.shape[1]
    total = TILE * TILES
    shape = jax.ShapeDtypeStruct
    dma = pltpu.SemaphoreType.DMA
    groups = len(GROUPS)
    vmem = pltpu.VMEM
    scratch = [
        vmem((comps + 2 * HALF, ROWS, COLS), f32),
        vmem((total, units), b16),
        vmem((units, total), b16),
        vmem((TILES, 8, TILE), f32),
        vmem(ocean.shape, f32),
        vmem(wind.shape, f32),
        vmem(mask.shape, jnp.int32),
        vmem((ROWS, 2, HALF, COLS), f32),
        vmem((ROWS, 2, COLS, COLS), f32),
        vmem((TILES, ROWS + 2, HALF + 2 * PAD, TILE), f32),
        vmem((TILES, ROWS + 2, HALF + 2 * PAD, TILE), f32),
        vmem((TILES, CELLS, TILE), f32),
        vmem((TILES, CELLS, TILE), f32),
        vmem((CELLS, total), b16),
        vmem((CELLS, units), f32),
        vmem((CELLS, units), b16),
        vmem((4, CELLS, TILE), f32),
        vmem((5, CELLS, TILE), f32),
        vmem((CELLS, TILE), f32),
        vmem((CELLS, TILE), f32),
        vmem((CELLS, TILE), f32),
        vmem((TILE, TILE), f32),
        vmem((TILE, TILE), f32),
        vmem((2, TILES, HALF, TILE), b16),
        vmem((2, TILES, HALF, TILE), b16),
        vmem((2, OWN + 1, HALF, TILE), b16),
        vmem((2, OWN + 1, HALF, TILE), b16),
        vmem((2, OWN + 1, HALF, TILE), b16),
        *[vmem((24, TILE), f32) for _ in range(7)],
        vmem((2, TILES, HALF, TILE), b16),
        vmem((2, TILES, HALF, TILE), b16),
        *[vmem((2, 24, TILE), f32) for _ in range(4)],
        vmem((2, 64, COLS), f32),
        vmem((2, 64, COLS), f32),
        vmem((256, COLS), f32),
        vmem((COLS, 256), f32),
        vmem((2, COLS, 256), f32),
        vmem((8, COLS), f32),
        vmem((8, COLS), f32),
        vmem((8, COLS), f32),
        vmem((2, 8, COLS), f32),
        vmem((2, 8, COLS), f32),
        vmem((2, TILES, HALF, TILE), b16),
        vmem((2, TILES, HALF, TILE), b16),
        vmem((OWN + 1, CELLS, TILE), f32),
        pltpu.SMEM((2, 1, ROWS), jnp.int32),
        pltpu.SMEM((2, 1, ROWS), jnp.int32),
        dma((16,)),
        dma((2,)), dma((2,)),
        dma((2,)), dma((2,)),
        dma((2, 4)), dma((2, 4)),
        dma((2,)), dma((2,)),
        dma((2, 2)), dma((2, 2)),
        dma((3,)), dma((3,)),
        dma((2, groups)), dma((2, groups)),
        dma((2, groups)), dma((2, groups)),
        dma((5,)), dma((5,)),
        dma((2, 3)), dma((2, 3)),
    ]
    return pl.pallas_call(
        kernel,
        out_shape=(shape(spectra.shape, f32), shape(ocean.shape, f32)),
        in_specs=[pl.BlockSpec(memory_space=pl.ANY)] * 11,
        out_specs=(pl.BlockSpec(memory_space=pltpu.VMEM),) * 2,
        scratch_shapes=scratch,
        compiler_params=pltpu.CompilerParams(
            vmem_limit_bytes=VMEM_LIMIT, collective_id=0, has_side_effects=True
        ),
    )(*(
        pltpu.with_memory_space_constraint(x, pltpu.HBM)
        for x in (
            spectra, first, second, table, ocean, wind, mask, cblocks, sblocks, crows, srows
        )
    ))


PIECES = 4


def place_kernel(a, b, a_out, b_out, sems):
    rows = a.shape[0] // PIECES
    copies = [pltpu.make_async_copy(b, b_out, sems.at[PIECES])]
    for n in range(PIECES):
        part = pl.ds(n * rows, rows)
        copies.append(pltpu.make_async_copy(a.at[part], a_out.at[part], sems.at[n]))
    for copy in copies:
        copy.start()
    for copy in copies:
        copy.wait()


def place_call(a, b):
    shape = jax.ShapeDtypeStruct
    return pl.pallas_call(
        place_kernel,
        out_shape=(shape(a.shape, a.dtype), shape(b.shape, b.dtype)),
        in_specs=[pl.BlockSpec(memory_space=pl.ANY)] * 2,
        out_specs=(pl.BlockSpec(memory_space=pl.ANY),) * 2,
        scratch_shapes=[pltpu.SemaphoreType.DMA((PIECES + 1,))],
        compiler_params=pltpu.CompilerParams(vmem_limit_bytes=VMEM_LIMIT),
    )(a, b)


def local_step(
    spectra,
    wind_field,
    sea_mask,
    first_layer,
    second_layer,
    ocean_state,
    current_blocks,
    current_rows,
    stress_blocks,
    stress_rows,
):
    half_freqs, directions, rows, cols = spectra.shape
    variables, levels = ocean_state.shape[:2]
    table = jnp.asarray(tables(2 * half_freqs, directions))
    state, ocean = kernel_call(
        spectra.reshape(half_freqs * directions, rows, cols),
        first_layer,
        second_layer,
        table,
        ocean_state.reshape(variables * levels, rows, cols),
        wind_field,
        sea_mask,
        current_blocks,
        stress_blocks,
        current_rows.transpose(1, 2, 0),
        stress_rows.transpose(1, 2, 0),
    )
    state, ocean = place_call(state, ocean)
    return state.reshape(spectra.shape), ocean.reshape(ocean_state.shape)


def solution(mesh):
    placed = (
        P("comp", None, "gy", "gx"),
        P(None, "gy", "gx"),
        P("gy", "gx"),
        P(),
        P(),
        P(None, None, "gy", "gx"),
        P("gy", None, "gx", None),
        P("gy", None, "gx"),
        P("gy", None, "gx", None),
        P("gy", None, "gx"),
    )
    return jax.shard_map(
        local_step,
        mesh=mesh,
        in_specs=placed,
        out_specs=(P("comp", None, "gy", "gx"), P(None, None, "gy", "gx")),
        check_vma=False,
    )
```
